256 devices in a mesh: dp: 4 (over x), mp: 64 (over z, y, core).
Axes of the slice: x: 4, y: 4, z: 8, core: 2. Of those that a mesh axis runs over, the one named last changes fastest.
Arguments:
- partial_grads: bfloat16 [4, 224, 512, 512], P('dp', None, 'mp'), may hold values from -3 to 3
- stat_left: float32 [4, 128, 512, 512], P('dp', 'mp'), as said below
- stat_right: float32 [4, 128, 512, 512], P('dp', 'mp'), as said below
- assign: int32 [224], replicated, may hold values from 0 to 511, as said below
- query_vectors: bfloat16 [1024, 8192], P('dp', 'mp'), may hold values from -36 to 36
- key_vectors: bfloat16 [1024, 8192], P('dp', 'mp'), may hold values from -36 to 36
- value_vectors: bfloat16 [1024, 8192], P('dp', 'mp'), may hold values from -6 to 6
Outputs:
- left_next: float32 [4, 128, 512, 512], P('dp', 'mp')
- right_next: float32 [4, 128, 512, 512], P('dp', 'mp')
- update: bfloat16 [224, 512, 512], P(None, 'mp')
- attended: bfloat16 [1024, 8192], P('dp', 'mp')
The draws below stay inside these ranges and needn't reach their ends.
Inputs may be any that keep to these rules, and one draw needn't show every extreme that they name: `assign`: distinct values: no slot holds two blocks; in every draw all 2 slots of some device hold blocks. `stat_left`: each slot's matrix is symmetric and positive definite. `stat_right`: each slot's matrix is symmetric and positive definite.
All inputs are finite; a program needn't handle non-finite values.
Results may differ from the reference program's by a relative error of at most 0.014.
Values may be sent and summed in bfloat16 or wider, within the bound.
A program may use at most 128 MiB of HBM per device.

```python
import math
import jax
import jax.numpy as jnp
from jax import lax

B = 512
CAP_DEV = 2
ITERS = 2
HEADS = 64
HD = 128
SEQ = 256
NBLK = 224
SLOTS = 512
TOKENS = 1024
N_DP = 4


def spd_stat(key, spread):
    key_one, key_two, key_three = jax.random.split(key, 3)
    raw = jax.random.uniform(key_one, (SLOTS, B, B), jnp.float32, -1.0, 1.0)
    symmetric = (raw + jnp.swapaxes(raw, 1, 2)) * (0.5 / B)
    diagonal = jax.random.uniform(key_two, (SLOTS, B, 1), jnp.float32, 1.5, 3.0)
    scales = jnp.exp(jax.random.uniform(key_three, (SLOTS, B, 1), jnp.float32, 0.0, spread))
    identity = (lax.broadcasted_iota(jnp.int32, (B, B), 0) == lax.broadcasted_iota(jnp.int32, (B, B), 1)).astype(jnp.float32)
    core = symmetric + identity[None] * diagonal
    whole = scales * core * jnp.swapaxes(scales, 1, 2)
    return whole.reshape(N_DP, SLOTS // N_DP, B, B).astype(jnp.float32)


def draw_stat_left(key, part):
    key = jax.random.fold_in(key, 21)
    return spd_stat(key, math.log(4.0))


def draw_stat_right(key, part):
    key = jax.random.fold_in(key, 22)
    return spd_stat(key, math.log(4.0))


def draw_assign(key, part):
    key = jax.random.fold_in(key, 23)
    key_one, key_two, key_three = jax.random.split(key, 3)
    owners = SLOTS // CAP_DEV
    filled = jax.random.randint(key_one, (), 0, owners)
    rotated = (jnp.arange(SLOTS, dtype=jnp.int32) + filled * CAP_DEV) % SLOTS
    others = CAP_DEV + jax.random.permutation(key_two, SLOTS - CAP_DEV)
    chosen = jnp.concatenate([rotated[:CAP_DEV], rotated[others[:NBLK - CAP_DEV]]])
    shuffled = jax.random.permutation(key_three, NBLK)
    return chosen[shuffled].astype(jnp.int32)


def draw_query_vectors(key, part):
    key = jax.random.fold_in(key, 31)
    base = jnp.clip(jax.random.normal(key, (TOKENS // SEQ, SEQ, HEADS, HD), jnp.float32), -6.0, 6.0)
    return base.reshape(TOKENS, HEADS * HD).astype(jnp.bfloat16)


def draw_key_vectors(key, part):
    key = jax.random.fold_in(key, 41)
    base = jnp.clip(jax.random.normal(key, (TOKENS // SEQ, SEQ, HEADS, HD), jnp.float32), -6.0, 6.0)
    return base.reshape(TOKENS, HEADS * HD).astype(jnp.bfloat16)


def block_levels(key, extent, cuts, low, high):
    def one(axis_at, shards_of):
        steps = jax.random.uniform(jax.random.fold_in(jax.random.fold_in(key, 6), axis_at), (shards_of,), jnp.float32, low / len(cuts), high / len(cuts))
        return jnp.repeat(jnp.exp(steps), extent[axis_at] // shards_of).reshape((-1,) + (1,) * (len(extent) - axis_at - 1))

    gain = one(*cuts[0])
    for cut in cuts[1:]:
        gain = gain * one(*cut)
    return gain


def bell_draw(own_key, dims, scale, limit, pieces=(), held_as=jnp.bfloat16):
    drawn = jax.random.normal(own_key, dims, jnp.float32) * scale
    if len(pieces) > 0:
        drawn = block_levels(own_key, dims, pieces, -0.22, 0.18) * drawn
    return jnp.clip(drawn, min=-limit, max=limit).astype(held_as)


def setup_inputs(seed: int = 0) -> dict:
    keys = jax.random.split(jax.random.key(seed), 8)
    partial_grads = bell_draw(keys[0], (N_DP, NBLK, B, B), 0.5, 3.0, ((0, 4), (2, 64)))
    stat_left = draw_stat_left(jax.random.fold_in(keys[7], 71), 0)
    stat_right = draw_stat_right(jax.random.fold_in(keys[7], 71), 0)
    assign = draw_assign(jax.random.fold_in(keys[7], 71), 0)
    query_vectors = draw_query_vectors(jax.random.fold_in(keys[7], 71), 0)
    key_vectors = draw_key_vectors(jax.random.fold_in(keys[7], 71), 0)
    value_vectors = bell_draw(keys[6], (TOKENS, HEADS * HD), 1.0, 6.0, ((0, 4), (1, 64)))
    return dict(partial_grads=partial_grads, stat_left=stat_left, stat_right=stat_right, assign=assign, query_vectors=query_vectors, key_vectors=key_vectors, value_vectors=value_vectors)


BETA = 0.9

def product(left, right):
    return jnp.matmul(left, right, precision=lax.Precision.HIGHEST)

def inverse_root(matrix):
    identity = jnp.eye(matrix.shape[-1], dtype=jnp.float32)
    norm_size = jnp.sqrt(lax.optimization_barrier(jnp.sum(matrix * matrix, axis=(-2, -1), keepdims=True)) + 1e-06)
    scaled = matrix / norm_size
    root = identity
    for iteration in range(ITERS):
        factor = (5.0 * identity - scaled) * 0.25
        if iteration == 0:
            root = factor
        else:
            root = product(root, factor)
        if iteration + 1 < ITERS:
            squared = product(factor, factor)
            scaled = product(product(squared, squared), scaled)
    return root

def precondition(block, left_stat, right_stat):
    widened = block.astype(jnp.float32)
    raw = product(product(inverse_root(left_stat), widened), inverse_root(right_stat))
    ratio = (jnp.mean(widened * widened) + 1e-06) / (jnp.mean(raw * raw) + 1e-06)
    return (raw * jnp.sqrt(ratio)).astype(jnp.bfloat16)

def attend(packed):
    query_block, key_block, value_block = packed
    scale = 1.0 / math.sqrt(query_block.shape[-1])
    scores = jnp.einsum('qhd,khd->hqk', query_block.astype(jnp.float32), key_block.astype(jnp.float32)) * scale
    length = scores.shape[-1]
    causal = lax.broadcasted_iota(jnp.int32, (length, length), 0) >= lax.broadcasted_iota(jnp.int32, (length, length), 1)
    scores = jnp.where(causal[None], scores, -jnp.inf)
    highest = lax.optimization_barrier(jnp.max(scores, axis=-1, keepdims=True))
    weights = jnp.exp(scores - highest)
    probs = (weights / lax.optimization_barrier(jnp.sum(weights, axis=-1, keepdims=True))).astype(jnp.bfloat16)
    mixed = jnp.einsum('hqk,khd->qhd', probs.astype(jnp.float32), value_block.astype(jnp.float32))
    return mixed.astype(jnp.bfloat16)

def reference(partial_grads, stat_left, stat_right, assign, query_vectors, key_vectors, value_vectors):
    gradient = lax.optimization_barrier(jnp.sum(partial_grads.astype(jnp.float32), axis=0)).astype(jnp.bfloat16)
    total_slots = stat_left.shape[0] * stat_left.shape[1]
    order = stat_left.shape[2]
    left_flat = stat_left.reshape(total_slots, order, order)
    right_flat = stat_right.reshape(total_slots, order, order)
    source = jnp.full((total_slots,), -1, jnp.int32).at[assign].set(jnp.arange(assign.shape[0], dtype=jnp.int32))

    def slot_stats(packed):
        index, left_stat, right_stat = packed
        block = jnp.where(index >= 0, gradient[jnp.maximum(index, 0)], jnp.zeros((order, order), jnp.bfloat16))
        left_gram = jnp.dot(block, block.T, preferred_element_type=jnp.float32)
        right_gram = jnp.dot(block.T, block, preferred_element_type=jnp.float32)
        return (BETA * left_stat + (1.0 - BETA) * left_gram, BETA * right_stat + (1.0 - BETA) * right_gram)
    left_next, right_next = lax.map(slot_stats, (source, left_flat, right_flat))

    def block_update(packed):
        block, slot_index = packed
        return precondition(block, left_next[slot_index], right_next[slot_index])
    update = lax.map(block_update, (gradient, assign))
    sequences = query_vectors.shape[0] // SEQ
    shaped = (sequences, SEQ, HEADS, HD)
    attended = lax.map(attend, (query_vectors.reshape(shaped), key_vectors.reshape(shaped), value_vectors.reshape(shaped)))
    attended = attended.reshape(query_vectors.shape)
    return (left_next.reshape(stat_left.shape), right_next.reshape(stat_right.shape), update, attended)
```

```python
import math

import jax
import jax.numpy as jnp
from jax import lax
from jax.sharding import PartitionSpec as P

HD = 128


BETA = 0.9


def narrow(left, right):
    return jnp.matmul(
        left.astype(jnp.bfloat16), right.astype(jnp.bfloat16), preferred_element_type=jnp.float32
    )


def root_excess(matrix):
    norm_size = jnp.sqrt(jnp.sum(matrix * matrix, axis=(-2, -1), keepdims=True) + 1e-06)
    first = matrix / norm_size
    second = narrow(first, first)
    third = narrow(second, first)
    tail = (250.0 * first - 25.0 * second + third) * (1.0 / 4096.0)
    return (
        -(5.0 / 16.0 + 3125.0 / 4096.0) * first
        + (3125.0 / 4096.0) * second
        - (1250.0 / 4096.0) * third
        + narrow(tail, third)
    )


def precondition(block, left_stat, right_stat):
    widened = block.astype(jnp.float32)
    half = (25.0 / 16.0) * widened + narrow(root_excess(left_stat), block)
    raw = (25.0 / 16.0) * half + narrow(half, root_excess(right_stat))
    ratio = (jnp.mean(widened * widened) + 1e-06) / (jnp.mean(raw * raw) + 1e-06)
    return (raw * jnp.sqrt(ratio)).astype(jnp.bfloat16)


def local_attention(query_vectors, key_vectors, value_vectors):
    length = query_vectors.shape[0]
    local_heads = query_vectors.shape[1] // HD
    shaped = (length, local_heads, HD)
    queries = query_vectors.reshape(shaped)
    keys_local = key_vectors.reshape(shaped)
    values_local = value_vectors.reshape(shaped)
    scale = 1.0 / math.sqrt(HD)
    scores = (
        jnp.einsum("qhd,khd->hqk", queries, keys_local, preferred_element_type=jnp.float32) * scale
    )
    causal = lax.broadcasted_iota(jnp.int32, (length, length), 0) >= lax.broadcasted_iota(
        jnp.int32, (length, length), 1
    )
    scores = jnp.where(causal[None], scores, -jnp.inf)
    highest = jnp.max(scores, axis=-1, keepdims=True)
    weights = jnp.exp(scores - highest)
    probs = (weights / jnp.sum(weights, axis=-1, keepdims=True)).astype(jnp.bfloat16)
    mixed = jnp.einsum("hqk,khd->qhd", probs, values_local, preferred_element_type=jnp.float32)
    return mixed.astype(jnp.bfloat16).reshape(query_vectors.shape)


def body(partial_grads, stat_left, stat_right, assign, query_vectors, key_vectors, value_vectors):
    replica_count = lax.axis_size("dp")
    column_count = lax.axis_size("mp")
    capacity = stat_left.shape[1]
    block_order = partial_grads.shape[3]
    sliver_rows = partial_grads.shape[2]
    total_slots = replica_count * column_count * capacity
    block_count = assign.shape[0]
    source = (
        jnp.full((total_slots,), -1, jnp.int32)
        .at[assign]
        .set(jnp.arange(block_count, dtype=jnp.int32))
    )
    picked = jnp.take(partial_grads[0], jnp.maximum(source, 0), axis=0)
    packed = jnp.where((source >= 0)[:, None, None], picked, jnp.zeros((), jnp.bfloat16))
    grouped = packed.astype(jnp.float32).reshape(
        replica_count, column_count * capacity, sliver_rows, block_order
    )
    summed = lax.psum_scatter(grouped.astype(jnp.bfloat16), "dp", scatter_dimension=0, tiled=True)
    rounded = summed.reshape(column_count, capacity, sliver_rows, block_order)
    owned = lax.all_to_all(rounded, "mp", split_axis=0, concat_axis=2, tiled=True)[0]
    left_gram = jnp.einsum("sik,sjk->sij", owned, owned, preferred_element_type=jnp.float32)
    right_gram = jnp.einsum("ski,skj->sij", owned, owned, preferred_element_type=jnp.float32)
    left_next = BETA * stat_left[0] + (1.0 - BETA) * left_gram
    right_next = BETA * stat_right[0] + (1.0 - BETA) * right_gram
    attended = local_attention(query_vectors, key_vectors, value_vectors)
    updates = jax.vmap(precondition)(owned, left_next, right_next)
    returned = lax.all_to_all(updates, "mp", split_axis=1, concat_axis=0, tiled=True)
    everywhere = lax.all_gather(returned, "dp", axis=0, tiled=True)
    update = jnp.take(everywhere, assign, axis=0)
    return (left_next[None], right_next[None], update, attended)


def solution(mesh):
    placed = (
        P("dp", None, "mp", None),
        P("dp", "mp", None, None),
        P("dp", "mp", None, None),
        P(),
        P("dp", "mp"),
        P("dp", "mp"),
        P("dp", "mp"),
    )
    return jax.shard_map(
        body,
        mesh=mesh,
        in_specs=placed,
        out_specs=(
            P("dp", "mp", None, None),
            P("dp", "mp", None, None),
            P(None, "mp", None),
            P("dp", "mp"),
        ),
        check_vma=False,
    )
```

```python
import functools
import math

import jax
import jax.numpy as jnp
from jax import lax
from jax.experimental import pallas as pl
from jax.experimental.pallas import tpu as pltpu
from jax.sharding import PartitionSpec as P

HD = 128
BETA = 0.9
MESH = pl.DeviceIdType.MESH
VMEM = pltpu.VMEM
SMEM = pltpu.SMEM


def narrow(left, right):
    return jnp.matmul(
        left.astype(jnp.bfloat16), right.astype(jnp.bfloat16), preferred_element_type=jnp.float32
    )


def root_excess(matrix):
    norm_size = jnp.sqrt(jnp.sum(matrix * matrix, axis=(-2, -1), keepdims=True) + 1e-06)
    first = matrix / norm_size
    second = narrow(first, first)
    third = narrow(second, first)
    tail = (250.0 * first - 25.0 * second + third) * (1.0 / 4096.0)
    return (
        -(5.0 / 16.0 + 3125.0 / 4096.0) * first
        + (3125.0 / 4096.0) * second
        - (1250.0 / 4096.0) * third
        + narrow(tail, third)
    )


def precondition(block, left_stat, right_stat):
    widened = block.astype(jnp.float32)
    half = (25.0 / 16.0) * widened + narrow(root_excess(left_stat), block)
    raw = (25.0 / 16.0) * half + narrow(half, root_excess(right_stat))
    ratio = (jnp.mean(widened * widened) + 1e-06) / (jnp.mean(raw * raw) + 1e-06)
    return (raw * jnp.sqrt(ratio)).astype(jnp.bfloat16)


def local_attention(query_vectors, key_vectors, value_vectors):
    length = query_vectors.shape[0]
    local_heads = query_vectors.shape[1] // HD
    shaped = (length, local_heads, HD)
    queries = query_vectors.reshape(shaped)
    keys_local = key_vectors.reshape(shaped)
    values_local = value_vectors.reshape(shaped)
    scale = 1.0 / math.sqrt(HD)
    scores = (
        jnp.einsum("qhd,khd->hqk", queries, keys_local, preferred_element_type=jnp.float32) * scale
    )
    causal = lax.broadcasted_iota(jnp.int32, (length, length), 0) >= lax.broadcasted_iota(
        jnp.int32, (length, length), 1
    )
    scores = jnp.where(causal[None], scores, -jnp.inf)
    highest = jnp.max(scores, axis=-1, keepdims=True)
    weights = jnp.exp(scores - highest)
    probs = (weights / jnp.sum(weights, axis=-1, keepdims=True)).astype(jnp.bfloat16)
    mixed = jnp.einsum("hqk,khd->qhd", probs, values_local, preferred_element_type=jnp.float32)
    return mixed.astype(jnp.bfloat16).reshape(query_vectors.shape)


def to_slab(rows):
    half = rows.shape[1] // 2
    return jnp.concatenate([rows[:, :half], rows[:, half:]], axis=0)


def from_slab(slab):
    half = slab.shape[0] // 2
    return jnp.concatenate([slab[:half], slab[half:]], axis=1)


def loop(count, body, unroll=1):
    def step(index, carry):
        body(index)
        return carry

    lax.fori_loop(0, count, step, 0, unroll=unroll)


class Ring:
    def __init__(self, caps):
        self.caps = caps
        self.total = sum(caps)
        here = lax.axis_index("dp")
        self.right = {"dp": lax.rem(here + 1, 4)}
        self.left = {"dp": lax.rem(here + 3, 4)}

    def halves(self, chunk):
        first = self.caps[chunk] // 2
        return pl.ds(0, first), pl.ds(first, self.caps[chunk] - first)

    def start(self, chunk):
        return sum(self.caps[:chunk])


def remote(src, dst, send_sem, recv_sem, device):
    return pltpu.make_async_remote_copy(
        src_ref=src, dst_ref=dst, send_sem=send_sem, recv_sem=recv_sem, device_id=device, device_id_type=MESH
    )


def peer_of(me, step, count):
    if count != 64:
        return lax.rem(me + step, count)
    z, y, core = me // 8, (me // 2) % 4, me % 2
    z = lax.rem(z + lax.rem(step, 8) * 3, 8)
    y = lax.rem(y + lax.rem(step // 8, 4), 4)
    core = lax.rem(core + step // 32, 2)
    return z * 8 + y * 2 + core


def greet(ring, count):
    barrier = pltpu.get_barrier_semaphore()
    me = lax.axis_index("mp")
    for device in (ring.left, ring.right):
        pl.semaphore_signal(barrier, inc=1, device_id=device, device_id_type=MESH)

    def signal(step):
        pl.semaphore_signal(
            barrier, inc=1, device_id={"mp": peer_of(me, step + 1, count)}, device_id_type=MESH
        )

    loop(count - 1, signal)
    pl.semaphore_wait(barrier, count + 1)


def exchange_start(src, dst, send_sem, recv_sem, count):
    me = lax.axis_index("mp")

    def send(step):
        peer = peer_of(me, step + 1, count)
        remote(src.at[peer], dst.at[me], send_sem, recv_sem, {"mp": peer}).start()

    loop(count - 1, send)
    pltpu.make_async_copy(src.at[me], dst.at[me], recv_sem).start()


def exchange_wait_recv(dst, recv_sem):
    pltpu.make_async_copy(dst, dst, recv_sem).wait()


def exchange_wait_send(src, send_sem, count):
    part = src.at[pl.ds(0, count - 1)]
    pltpu.make_async_copy(part, part, send_sem).wait()


def scatter_copies(ring, chunk, buffers, send, recv):
    first, second = ring.halves(chunk)
    xs, tl, tr, fl, fr = buffers
    plan = (
        (xs.at[2, first], tl.at[first], ring.right),
        (xs.at[2, second], tr.at[second], ring.left),
        (xs.at[1, second], fl.at[second], ring.right),
        (xs.at[3, first], fr.at[first], ring.left),
        (xs.at[1, first], fl.at[first], ring.right),
        (xs.at[3, second], fr.at[second], ring.left),
    )
    return [remote(s, t, send.at[chunk, k], recv.at[chunk, k], to) for k, (s, t, to) in enumerate(plan)]


def gather_copies(ring, chunk, q, send, recv):
    first, second = (
        pl.ds(ring.start(chunk) + part.start, part.size) for part in ring.halves(chunk)
    )
    plan = (
        (q.at[0, first], q.at[3, first], ring.right),
        (q.at[0, second], q.at[1, second], ring.left),
        (q.at[0, second], q.at[3, second], ring.right),
        (q.at[0, first], q.at[1, first], ring.left),
        (q.at[3, first], q.at[2, first], ring.right),
        (q.at[1, second], q.at[2, second], ring.left),
    )
    return [remote(s, t, send.at[chunk, k], recv.at[chunk, k], to) for k, (s, t, to) in enumerate(plan)]


def collect_kernel(
    caps, count, src_ref, dense_ref, grads_ref, owned_ref,
    *scratch,
):
    buffers = (scratch[:5], scratch[5:10])
    out_slabs = scratch[10:12]
    in_slabs = scratch[12:14]
    x_send, x_recv, a_send, a_recv = scratch[14:]
    ring = Ring(caps)
    total = ring.total
    here = lax.axis_index("dp")
    greet(ring, count)

    def pack(chunk, relative, part):
        base = lax.rem(here + relative, 4) * total + ring.start(chunk) + part.start
        xs = buffers[chunk][0]

        def one(index):
            block = src_ref[base + index]
            xs[relative, part.start + index] = to_slab(grads_ref[block].astype(jnp.float32)).astype(jnp.bfloat16)

        loop(part.size, one, unroll=4)

    def add(chunk, relative, arrived, part):
        xs = buffers[chunk][0]

        def one(index):
            at = part.start + index
            both = xs[relative, at].astype(jnp.float32) + arrived[at].astype(jnp.float32)
            xs[relative, at] = both.astype(jnp.bfloat16)

        loop(part.size, one, unroll=4)

    copies = [scatter_copies(ring, chunk, buffers[chunk], x_send, x_recv) for chunk in range(2)]

    def open_chunk(chunk):
        first, second = ring.halves(chunk)
        for relative, part, copy in ((2, first, 0), (2, second, 1), (1, second, 2), (3, first, 3)):
            pack(chunk, relative, part)
            copies[chunk][copy].start()
        pack(chunk, 1, first)
        pack(chunk, 3, second)

    def relay(chunk):
        first, second = ring.halves(chunk)
        copies[chunk][0].wait_recv()
        add(chunk, 1, buffers[chunk][1], first)
        copies[chunk][4].start()
        copies[chunk][1].wait_recv()
        add(chunk, 3, buffers[chunk][2], second)
        copies[chunk][5].start()

    def finish(chunk):
        for copy in range(2, 6):
            copies[chunk][copy].wait_recv()
        xs, _, _, fl, fr = buffers[chunk]

        def one(owner):
            place = dense_ref[chunk * count + owner]
            at = jnp.maximum(place, 0)
            whole = xs[0, at].astype(jnp.float32) + fl[at].astype(jnp.float32) + fr[at].astype(jnp.float32)
            out_slabs[chunk][owner] = jnp.where(place >= 0, whole, 0.0).astype(jnp.bfloat16)

        loop(count, one, unroll=4)
        exchange_start(out_slabs[chunk], in_slabs[chunk], a_send.at[chunk], a_recv.at[chunk], count)

    open_chunk(0)
    relay(0)
    open_chunk(1)
    for chunk in range(2):
        for part in ring.halves(chunk):
            pack(chunk, 0, part)
    finish(0)
    relay(1)
    finish(1)

    for chunk in range(2):
        exchange_wait_recv(in_slabs[chunk], a_recv.at[chunk])

        def place(pair):
            upper = from_slab(in_slabs[chunk][2 * pair].astype(jnp.float32))
            lower = from_slab(in_slabs[chunk][2 * pair + 1].astype(jnp.float32))
            rows = pl.ds(pl.multiple_of(pair * 16, 16), 16)
            owned_ref[chunk, rows] = jnp.concatenate([upper, lower], axis=0).astype(jnp.bfloat16)

        loop(count // 2, place, unroll=2)
    for chunk in range(2):
        for copy in copies[chunk]:
            copy.wait_send()
        exchange_wait_send(out_slabs[chunk], a_send.at[chunk], count)


def collect(grads, src, dense, caps, count):
    total = sum(caps)
    blocks, rows, columns = grads.shape
    slab = (2 * rows, columns // 2)
    return pl.pallas_call(
        functools.partial(collect_kernel, caps, count),
        out_shape=jax.ShapeDtypeStruct((2, count * rows, columns), jnp.bfloat16),
        in_specs=[pl.BlockSpec(memory_space=SMEM)] * 2 + [pl.BlockSpec(memory_space=VMEM)],
        out_specs=pl.BlockSpec(memory_space=VMEM),
        scratch_shapes=[
            *[
                VMEM(lead + slab, jnp.bfloat16)
                for cap in caps
                for lead in ((4, cap), (cap,), (cap,), (cap,), (cap,))
            ],
            *[VMEM((count,) + slab, jnp.bfloat16)] * 4,
            pltpu.SemaphoreType.DMA((2, 6)),
            pltpu.SemaphoreType.DMA((2, 6)),
            pltpu.SemaphoreType.DMA((2,)),
            pltpu.SemaphoreType.DMA((2,)),
        ],
        compiler_params=pltpu.CompilerParams(
            collective_id=0, has_side_effects=True, vmem_limit_bytes=48 * 2**20
        ),
    )(src, dense, grads)


def spread_kernel(
    caps, count, packed_ref, place_ref, ready_ref, update_ref,
    *scratch,
):
    out_slabs, in_slabs = scratch[0:2], scratch[2:4]
    q, x_send, x_recv, a_send, a_recv = scratch[4:]
    ring = Ring(caps)
    greet(ring, count)
    for chunk in range(2):

        def cut(pair):
            rows = pl.ds(pl.multiple_of(pair * 16, 16), 16)
            both = ready_ref[chunk, rows].astype(jnp.float32)
            out_slabs[chunk][2 * pair] = to_slab(both[:8]).astype(jnp.bfloat16)
            out_slabs[chunk][2 * pair + 1] = to_slab(both[8:]).astype(jnp.bfloat16)

        loop(count // 2, cut, unroll=2)
        exchange_start(out_slabs[chunk], in_slabs[chunk], a_send.at[chunk], a_recv.at[chunk], count)

    copies = [gather_copies(ring, chunk, q, x_send, x_recv) for chunk in range(2)]

    def open_chunk(chunk):
        exchange_wait_recv(in_slabs[chunk], a_recv.at[chunk])
        first, second = ring.halves(chunk)
        for part, starts in ((first, (0, 3)), (second, (1, 2))):

            def one(index):
                at = ring.start(chunk) + part.start + index
                q[0, at] = in_slabs[chunk][packed_ref[at]]

            loop(part.size, one, unroll=4)
            for copy in starts:
                copies[chunk][copy].start()

    def forward(chunk):
        for arrived, onward in ((0, 4), (1, 5)):
            copies[chunk][arrived].wait_recv()
            copies[chunk][onward].start()

    open_chunk(0)
    forward(0)
    open_chunk(1)
    forward(1)
    for chunk in range(2):
        for copy in range(2, 6):
            copies[chunk][copy].wait_recv()

    def settle(block):
        place = place_ref[block]
        slab = q[place // ring.total, place % ring.total]
        update_ref[block] = from_slab(slab.astype(jnp.float32)).astype(jnp.bfloat16)

    loop(update_ref.shape[0], settle, unroll=4)
    for chunk in range(2):
        for copy in copies[chunk]:
            copy.wait_send()
        exchange_wait_send(out_slabs[chunk], a_send.at[chunk], count)


def spread(ready, packed, place, caps, count, rows):
    total = sum(caps)
    columns = ready.shape[2]
    slab = (2 * rows, columns // 2)
    return pl.pallas_call(
        functools.partial(spread_kernel, caps, count),
        out_shape=jax.ShapeDtypeStruct((place.shape[0], rows, columns), jnp.bfloat16),
        in_specs=[pl.BlockSpec(memory_space=SMEM)] * 2 + [pl.BlockSpec(memory_space=VMEM)],
        out_specs=pl.BlockSpec(memory_space=VMEM),
        scratch_shapes=[
            *[VMEM((count,) + slab, jnp.bfloat16)] * 4,
            VMEM((4, total) + slab, jnp.bfloat16),
            pltpu.SemaphoreType.DMA((2, 6)),
            pltpu.SemaphoreType.DMA((2, 6)),
            pltpu.SemaphoreType.DMA((2,)),
            pltpu.SemaphoreType.DMA((2,)),
        ],
        compiler_params=pltpu.CompilerParams(
            collective_id=1, has_side_effects=True, vmem_limit_bytes=48 * 2**20
        ),
    )(packed, place, ready)


def tables(assign, count):
    here = lax.axis_index("dp")
    total = 2 * count
    slots = 4 * total
    source = (
        jnp.full((slots,), -1, jnp.int32)
        .at[assign]
        .set(jnp.arange(assign.shape[0], dtype=jnp.int32))
    )
    ordered = source.reshape(4, count, 2).transpose(0, 2, 1).reshape(4, total)
    src = jnp.maximum(ordered, 0).reshape(slots)
    mine = lax.dynamic_index_in_dim(ordered, here, 0, keepdims=False)
    numbers = jnp.arange(total, dtype=jnp.int32)
    dense = jnp.where(mine >= 0, numbers % count, -1)
    packed = numbers % count
    replica, inside = assign // total, assign % total
    relative = (replica - here + 4) % 4
    place = relative * total + (inside % 2) * count + inside // 2
    return src, dense, packed, place


def body(partial_grads, stat_left, stat_right, assign, query_vectors, key_vectors, value_vectors):
    count = lax.axis_size("mp")
    caps = (count, count)
    src, dense, packed, place = tables(assign, count)
    owned = collect(partial_grads[0], src, dense, caps, count)
    left_gram = jnp.einsum("sik,sjk->sij", owned, owned, preferred_element_type=jnp.float32)
    right_gram = jnp.einsum("ski,skj->sij", owned, owned, preferred_element_type=jnp.float32)
    left_next = BETA * stat_left[0] + (1.0 - BETA) * left_gram
    right_next = BETA * stat_right[0] + (1.0 - BETA) * right_gram
    attended = local_attention(query_vectors, key_vectors, value_vectors)
    updates = jax.vmap(precondition)(owned, left_next, right_next)
    update = spread(updates, packed, place, caps, count, partial_grads.shape[2])
    return (left_next[None], right_next[None], update, attended)


def solution(mesh):
    placed = (
        P("dp", None, "mp", None),
        P("dp", "mp", None, None),
        P("dp", "mp", None, None),
        P(),
        P("dp", "mp"),
        P("dp", "mp"),
        P("dp", "mp"),
    )
    return jax.shard_map(
        body,
        mesh=mesh,
        in_specs=placed,
        out_specs=(
            P("dp", "mp", None, None),
            P("dp", "mp", None, None),
            P(None, "mp", None),
            P("dp", "mp"),
        ),
        check_vma=False,
    )
```

```python
import functools
import math

import jax
import jax.numpy as jnp
from jax import lax
from jax.experimental import pallas as pl
from jax.experimental.pallas import tpu as pltpu
from jax.sharding import PartitionSpec as P

BETA = 0.9
MESH = pl.DeviceIdType.MESH
VMEM = pltpu.VMEM
SMEM = pltpu.SMEM


def to_slab(rows):
    half = rows.shape[1] // 2
    return jnp.concatenate([rows[:, :half], rows[:, half:]], axis=0)


def from_slab(slab):
    half = slab.shape[0] // 2
    return jnp.concatenate([slab[:half], slab[half:]], axis=1)


def loop(count, body, unroll=1):
    def step(index, carry):
        body(index)
        return carry

    lax.fori_loop(0, count, step, 0, unroll=unroll)


class Ring:
    def __init__(self, caps):
        self.caps = caps
        self.total = sum(caps)
        here = lax.axis_index("dp")
        self.right = {"dp": lax.rem(here + 1, 4)}
        self.left = {"dp": lax.rem(here + 3, 4)}

    def halves(self, chunk):
        first = self.caps[chunk] // 2
        return pl.ds(0, first), pl.ds(first, self.caps[chunk] - first)

    def start(self, chunk):
        return sum(self.caps[:chunk])


def remote(src, dst, send_sem, recv_sem, device):
    return pltpu.make_async_remote_copy(
        src_ref=src, dst_ref=dst, send_sem=send_sem, recv_sem=recv_sem, device_id=device, device_id_type=MESH
    )


def peer_of(me, step, count):
    if count != 64:
        return lax.rem(me + step, count)
    z, y, core = me // 8, (me // 2) % 4, me % 2
    z = lax.rem(z + lax.rem(step, 8) * 3, 8)
    y = lax.rem(y + lax.rem(step // 8, 4), 4)
    core = lax.rem(core + step // 32, 2)
    return z * 8 + y * 2 + core


def greet(ring, count):
    barrier = pltpu.get_barrier_semaphore()
    me = lax.axis_index("mp")
    for device in (ring.left, ring.right):
        pl.semaphore_signal(barrier, inc=1, device_id=device, device_id_type=MESH)

    def signal(step):
        pl.semaphore_signal(
            barrier, inc=1, device_id={"mp": peer_of(me, step + 1, count)}, device_id_type=MESH
        )

    loop(count - 1, signal)
    pl.semaphore_wait(barrier, count + 1)


def exchange_start(src, dst, send_sem, recv_sem, count):
    me = lax.axis_index("mp")

    def send(step):
        peer = peer_of(me, step + 1, count)
        remote(src.at[peer], dst.at[me], send_sem, recv_sem, {"mp": peer}).start()

    loop(count - 1, send)
    pltpu.make_async_copy(src.at[me], dst.at[me], recv_sem).start()


def exchange_wait_recv(dst, recv_sem):
    pltpu.make_async_copy(dst, dst, recv_sem).wait()


def exchange_wait_send(src, send_sem, count):
    part = src.at[pl.ds(0, count - 1)]
    pltpu.make_async_copy(part, part, send_sem).wait()


def scatter_copies(ring, chunk, buffers, send, recv):
    first, second = ring.halves(chunk)
    xs, tl, tr, fl, fr = buffers
    plan = (
        (xs.at[2, first], tl.at[first], ring.right),
        (xs.at[2, second], tr.at[second], ring.left),
        (xs.at[1, second], fl.at[second], ring.right),
        (xs.at[3, first], fr.at[first], ring.left),
        (xs.at[1, first], fl.at[first], ring.right),
        (xs.at[3, second], fr.at[second], ring.left),
    )
    return [remote(s, t, send.at[chunk, k], recv.at[chunk, k], to) for k, (s, t, to) in enumerate(plan)]


def gather_copies(ring, chunk, q, send, recv):
    first, second = (
        pl.ds(ring.start(chunk) + part.start, part.size) for part in ring.halves(chunk)
    )
    plan = (
        (q.at[0, first], q.at[3, first], ring.right),
        (q.at[0, second], q.at[1, second], ring.left),
        (q.at[0, second], q.at[3, second], ring.right),
        (q.at[0, first], q.at[1, first], ring.left),
        (q.at[3, first], q.at[2, first], ring.right),
        (q.at[1, second], q.at[2, second], ring.left),
    )
    return [remote(s, t, send.at[chunk, k], recv.at[chunk, k], to) for k, (s, t, to) in enumerate(plan)]


LINEAR = -(5.0 / 16.0 + 3125.0 / 4096.0)
SQUARE = 3125.0 / 4096.0
CUBE = -1250.0 / 4096.0


def dot(left, right, dims=((1,), (0,))):
    return lax.dot_general(left, right, (dims, ((), ())), preferred_element_type=jnp.float32)


def column_parts(order, body):
    width = 256

    def one(part):
        body(pl.ds(pl.multiple_of(part * width, width), width))

    loop(order // width, one)


def excess(gram, stat, result, first_b, second, second_b, third_b, tail_b, out):
    order = stat.shape[0]

    def blend(columns):
        result[:, columns] = BETA * stat[:, columns] + (1.0 - BETA) * gram(columns)

    column_parts(order, blend)
    whole = result[...]
    scale = 1.0 / jnp.sqrt(jnp.sum(whole * whole) + 1e-06)
    first_b[...] = (result[...] * scale).astype(jnp.bfloat16)

    def square(columns):
        value = dot(first_b[...], first_b[:, columns])
        second[:, columns] = value
        second_b[:, columns] = value.astype(jnp.bfloat16)

    column_parts(order, square)

    def cube(columns):
        third = dot(second_b[...], first_b[:, columns])
        first = result[:, columns] * scale
        two = second[:, columns]
        third_b[:, columns] = third.astype(jnp.bfloat16)
        tail_b[:, columns] = ((250.0 * first - 25.0 * two + third) * (1.0 / 4096.0)).astype(jnp.bfloat16)
        second[:, columns] = LINEAR * first + SQUARE * two + CUBE * third

    column_parts(order, cube)

    def last(columns):
        out[:, columns] = (second[:, columns] + dot(tail_b[...], third_b[:, columns])).astype(jnp.bfloat16)

    column_parts(order, last)


def attend(query, key, value, out):
    length, width = query.shape
    scores = dot(query[...], key[...], ((1,), (1,))) * (1.0 / math.sqrt(width))
    causal = lax.broadcasted_iota(jnp.int32, (length, length), 0) >= lax.broadcasted_iota(
        jnp.int32, (length, length), 1
    )
    scores = jnp.where(causal, scores, -jnp.inf)
    weights = jnp.exp(scores - jnp.max(scores, axis=-1, keepdims=True))
    probs = (weights / jnp.sum(weights, axis=-1, keepdims=True)).astype(jnp.bfloat16)
    out[...] = dot(probs, value[...]).astype(jnp.bfloat16)


def step_kernel(
    caps, count, src_ref, dense_ref, packed_ref, place_ref,
    grads_ref, stat_left, stat_right, query, key, value,
    left_next, right_next, update_ref, attended,
    *scratch,
):
    buffers = (scratch[:5], scratch[5:10])
    out_slabs, in_slabs, out_back, in_back = scratch[10:12], scratch[12:14], scratch[14:16], scratch[16:18]
    q, block, first_b, second, second_b, third_b, tail_b, left_b, right_b, half_b = scratch[18:28]
    x_send, x_recv, a_send, a_recv, g_send, g_recv, b_send, b_recv = scratch[28:]
    ring = Ring(caps)
    total = ring.total
    here = lax.axis_index("dp")
    greet(ring, count)

    def pack(chunk, relative, part):
        base = lax.rem(here + relative, 4) * total + ring.start(chunk) + part.start
        xs = buffers[chunk][0]

        def one(index):
            number = src_ref[base + index]
            xs[relative, part.start + index] = to_slab(grads_ref[number].astype(jnp.float32)).astype(jnp.bfloat16)

        loop(part.size, one, unroll=4)

    def add(chunk, relative, arrived, part):
        xs = buffers[chunk][0]

        def one(index):
            at = part.start + index
            both = xs[relative, at].astype(jnp.float32) + arrived[at].astype(jnp.float32)
            xs[relative, at] = both.astype(jnp.bfloat16)

        loop(part.size, one, unroll=4)

    reduce = [scatter_copies(ring, chunk, buffers[chunk], x_send, x_recv) for chunk in range(2)]
    gather = [gather_copies(ring, chunk, q, g_send, g_recv) for chunk in range(2)]

    def open_chunk(chunk):
        first, second_half = ring.halves(chunk)
        for relative, part, copy in ((2, first, 0), (2, second_half, 1), (1, second_half, 2), (3, first, 3)):
            pack(chunk, relative, part)
            reduce[chunk][copy].start()
        pack(chunk, 1, first)
        pack(chunk, 3, second_half)

    def relay(chunk):
        first, second_half = ring.halves(chunk)
        reduce[chunk][0].wait_recv()
        add(chunk, 1, buffers[chunk][1], first)
        reduce[chunk][4].start()
        reduce[chunk][1].wait_recv()
        add(chunk, 3, buffers[chunk][2], second_half)
        reduce[chunk][5].start()

    def finish(chunk):
        for copy in range(2, 6):
            reduce[chunk][copy].wait_recv()
        xs, _, _, fl, fr = buffers[chunk]

        def one(owner):
            place = dense_ref[chunk * count + owner]
            at = jnp.maximum(place, 0)
            whole = xs[0, at].astype(jnp.float32) + fl[at].astype(jnp.float32) + fr[at].astype(jnp.float32)
            out_slabs[chunk][owner] = jnp.where(place >= 0, whole, 0.0).astype(jnp.bfloat16)

        loop(count, one, unroll=4)
        exchange_start(out_slabs[chunk], in_slabs[chunk], a_send.at[chunk], a_recv.at[chunk], count)

    def precondition(chunk):
        exchange_wait_recv(in_slabs[chunk], a_recv.at[chunk])

        def place(pair):
            upper = from_slab(in_slabs[chunk][2 * pair].astype(jnp.float32))
            lower = from_slab(in_slabs[chunk][2 * pair + 1].astype(jnp.float32))
            rows = pl.ds(pl.multiple_of(pair * 16, 16), 16)
            block[rows] = jnp.concatenate([upper, lower], axis=0).astype(jnp.bfloat16)

        loop(count // 2, place, unroll=2)
        order = block.shape[0]
        spare = (first_b, second, second_b, third_b, tail_b)
        excess(
            lambda columns: dot(block[...], block[columns], ((1,), (1,))),
            stat_left.at[chunk], left_next.at[chunk], *spare, left_b,
        )
        excess(
            lambda columns: dot(block[...], block[:, columns], ((0,), (0,))),
            stat_right.at[chunk], right_next.at[chunk], *spare, right_b,
        )

        def left_side(columns):
            part = (25.0 / 16.0) * block[:, columns].astype(jnp.float32) + dot(left_b[...], block[:, columns])
            second[:, columns] = part
            half_b[:, columns] = part.astype(jnp.bfloat16)

        column_parts(order, left_side)

        def right_side(columns):
            second[:, columns] = (25.0 / 16.0) * second[:, columns] + dot(half_b[...], right_b[:, columns])

        column_parts(order, right_side)
        raw = second[...]
        widened = block[...].astype(jnp.float32)
        mean_raw = jnp.sum(raw * raw) * (1.0 / raw.size)
        mean_block = jnp.sum(widened * widened) * (1.0 / raw.size)
        scale = jnp.sqrt((mean_block + 1e-06) / (mean_raw + 1e-06))

        def cut(owner):
            rows = pl.ds(pl.multiple_of(owner * 8, 8), 8)
            out_back[chunk][owner] = to_slab(second[rows] * scale).astype(jnp.bfloat16)

        loop(count, cut, unroll=4)
        exchange_start(out_back[chunk], in_back[chunk], b_send.at[chunk], b_recv.at[chunk], count)

    def open_gather(chunk):
        exchange_wait_recv(in_back[chunk], b_recv.at[chunk])
        for part, starts in zip(ring.halves(chunk), ((0, 3), (1, 2))):

            def one(index):
                at = ring.start(chunk) + part.start + index
                q[0, at] = in_back[chunk][packed_ref[at]]

            loop(part.size, one, unroll=4)
            for copy in starts:
                gather[chunk][copy].start()

    def forward(chunk):
        for arrived, onward in ((0, 4), (1, 5)):
            gather[chunk][arrived].wait_recv()
            gather[chunk][onward].start()

    open_chunk(0)
    attend(query, key, value, attended)
    relay(0)
    open_chunk(1)
    for chunk in range(2):
        for part in ring.halves(chunk):
            pack(chunk, 0, part)
    finish(0)
    relay(1)
    finish(1)
    precondition(0)
    precondition(1)
    open_gather(0)
    forward(0)
    open_gather(1)
    forward(1)
    for chunk in range(2):
        for copy in range(2, 6):
            gather[chunk][copy].wait_recv()

    def settle(number):
        place = place_ref[number]
        slab = q[place // total, place % total]
        update_ref[number] = from_slab(slab.astype(jnp.float32)).astype(jnp.bfloat16)

    loop(update_ref.shape[0], settle, unroll=4)
    for chunk in range(2):
        for copy in reduce[chunk] + gather[chunk]:
            copy.wait_send()
        exchange_wait_send(out_slabs[chunk], a_send.at[chunk], count)
        exchange_wait_send(out_back[chunk], b_send.at[chunk], count)


def step(grads, stat_left, stat_right, query, key, value, src, dense, packed, place, caps, count):
    total = sum(caps)
    blocks, rows, columns = grads.shape
    order = stat_left.shape[1]
    slab = (2 * rows, columns // 2)
    narrow = VMEM((order, order), jnp.bfloat16)
    wide = VMEM((order, order), jnp.float32)
    dma = pltpu.SemaphoreType.DMA
    return pl.pallas_call(
        functools.partial(step_kernel, caps, count),
        out_shape=(
            jax.ShapeDtypeStruct(stat_left.shape, jnp.float32),
            jax.ShapeDtypeStruct(stat_right.shape, jnp.float32),
            jax.ShapeDtypeStruct(grads.shape, jnp.bfloat16),
            jax.ShapeDtypeStruct(query.shape, jnp.bfloat16),
        ),
        in_specs=[pl.BlockSpec(memory_space=SMEM)] * 4 + [pl.BlockSpec(memory_space=VMEM)] * 6,
        out_specs=[pl.BlockSpec(memory_space=VMEM)] * 4,
        scratch_shapes=[
            *[
                VMEM(lead + slab, jnp.bfloat16)
                for cap in caps
                for lead in ((4, cap), (cap,), (cap,), (cap,), (cap,))
            ],
            *[VMEM((count,) + slab, jnp.bfloat16)] * 8,
            VMEM((4, total) + slab, jnp.bfloat16),
            narrow, narrow, wide, narrow, narrow, narrow, narrow, narrow, narrow,
            dma((2, 6)), dma((2, 6)), dma((2,)), dma((2,)),
            dma((2, 6)), dma((2, 6)), dma((2,)), dma((2,)),
        ],
        compiler_params=pltpu.CompilerParams(
            collective_id=0, has_side_effects=True, vmem_limit_bytes=56 * 2**20
        ),
    )(src, dense, packed, place, grads, stat_left, stat_right, query, key, value)


def tables(assign, count):
    here = lax.axis_index("dp")
    total = 2 * count
    slots = 4 * total
    source = (
        jnp.full((slots,), -1, jnp.int32)
        .at[assign]
        .set(jnp.arange(assign.shape[0], dtype=jnp.int32))
    )
    ordered = source.reshape(4, count, 2).transpose(0, 2, 1).reshape(4, total)
    src = jnp.maximum(ordered, 0).reshape(slots)
    mine = lax.dynamic_index_in_dim(ordered, here, 0, keepdims=False)
    numbers = jnp.arange(total, dtype=jnp.int32)
    dense = jnp.where(mine >= 0, numbers % count, -1)
    packed = numbers % count
    replica, inside = assign // total, assign % total
    relative = (replica - here + 4) % 4
    place = relative * total + (inside % 2) * count + inside // 2
    return src, dense, packed, place


def body(partial_grads, stat_left, stat_right, assign, query_vectors, key_vectors, value_vectors):
    count = lax.axis_size("mp")
    caps = (count, count)
    src, dense, packed, place = tables(assign, count)
    left_next, right_next, update, attended = step(
        partial_grads[0], stat_left[0], stat_right[0], query_vectors, key_vectors, value_vectors,
        src, dense, packed, place, caps, count,
    )
    return (left_next[None], right_next[None], update, attended)


def solution(mesh):
    placed = (
        P("dp", None, "mp", None),
        P("dp", "mp", None, None),
        P("dp", "mp", None, None),
        P(),
        P("dp", "mp"),
        P("dp", "mp"),
        P("dp", "mp"),
    )
    return jax.shard_map(
        body,
        mesh=mesh,
        in_specs=placed,
        out_specs=(
            P("dp", "mp", None, None),
            P("dp", "mp", None, None),
            P(None, "mp", None),
            P("dp", "mp"),
        ),
        check_vma=False,
    )
```

```python
import functools
import math

import jax
import jax.numpy as jnp
from jax import lax
from jax.experimental import pallas as pl
from jax.experimental.pallas import tpu as pltpu
from jax.sharding import PartitionSpec as P

BETA = 0.9
MESH = pl.DeviceIdType.MESH
VMEM = pltpu.VMEM
SMEM = pltpu.SMEM


def to_slab(rows):
    half = rows.shape[1] // 2
    return jnp.concatenate([rows[:, :half], rows[:, half:]], axis=0)


def from_slab(slab):
    half = slab.shape[0] // 2
    return jnp.concatenate([slab[:half], slab[half:]], axis=1)


def loop(count, body, unroll=1):
    def step(index, carry):
        body(index)
        return carry

    lax.fori_loop(0, count, step, 0, unroll=unroll)


class Place:
    def __init__(self, count):
        self.count = count
        self.pairs = count // 2
        self.deep, self.wide = (8, 4) if count == 64 else (count // 2, 1)
        self.replica = lax.axis_index("dp")
        self.me = lax.axis_index("mp")
        self.pair, self.core = self.me // 2, self.me % 2
        self.right = {"dp": lax.rem(self.replica + 1, 4)}
        self.left = {"dp": lax.rem(self.replica + 3, 4)}

    def partner(self, step):
        z, y = self.pair // self.wide, self.pair % self.wide
        z = lax.rem(z + lax.rem(step, self.deep) * 3, self.deep)
        y = lax.rem(y + step // self.deep, self.wide)
        return z * self.wide + y


CHUNKS = 4


def halves(cap):
    return pl.ds(0, cap // 2), pl.ds(cap // 2, cap - cap // 2)


def remote(src, dst, send_sem, recv_sem, device):
    return pltpu.make_async_remote_copy(
        src_ref=src, dst_ref=dst, send_sem=send_sem, recv_sem=recv_sem, device_id=device, device_id_type=MESH
    )


def greet(here):
    barrier = pltpu.get_barrier_semaphore()
    for device in (here.left, here.right, {"mp": here.pair * 2 + 1 - here.core}):
        pl.semaphore_signal(barrier, inc=1, device_id=device, device_id_type=MESH)

    def signal(step):
        for core in range(2):
            device = {"mp": here.partner(step + 1) * 2 + core}
            pl.semaphore_signal(barrier, inc=1, device_id=device, device_id_type=MESH)

    loop(here.pairs - 1, signal)
    pl.semaphore_wait(barrier, here.count + 1)


def hand_out(here, core, src, dst, send_sem, recv_sem):
    def send(pair):
        remote(src.at[pair], dst.at[here.me], send_sem, recv_sem, {"mp": pair * 2 + core}).start()

    @pl.when(here.core == core)
    def _():
        pltpu.make_async_copy(src.at[here.pair], dst.at[here.me], recv_sem).start()

    @pl.when(here.core != core)
    def _():
        send(here.pair)

    loop(here.pairs - 1, lambda step: send(here.partner(step + 1)))


def hand_back(here, src, dst, send_sem, recv_sem):
    def send(device):
        remote(src.at[device], dst.at[here.pair], send_sem, recv_sem, {"mp": device}).start()

    pltpu.make_async_copy(src.at[here.me], dst.at[here.pair], recv_sem).start()
    send(here.pair * 2 + 1 - here.core)

    def both(step):
        for core in range(2):
            send(here.partner(step + 1) * 2 + core)

    loop(here.pairs - 1, both)


def wait_all(ref, sem):
    pltpu.make_async_copy(ref, ref, sem).wait()


def scatter_copies(here, cap, buffers, send, recv):
    first, second = halves(cap)
    xs, tl, tr, fl, fr = buffers
    plan = (
        (xs.at[2, first], tl.at[first], here.right),
        (xs.at[2, second], tr.at[second], here.left),
        (xs.at[1, second], fl.at[second], here.right),
        (xs.at[3, first], fr.at[first], here.left),
        (xs.at[1, first], fl.at[first], here.right),
        (xs.at[3, second], fr.at[second], here.left),
    )
    return [remote(s, t, send.at[k], recv.at[k], to) for k, (s, t, to) in enumerate(plan)]


def gather_copies(here, cap, start, q, send, recv):
    first, second = (pl.ds(start + part.start, part.size) for part in halves(cap))
    plan = (
        (q.at[0, first], q.at[3, first], here.right),
        (q.at[0, second], q.at[1, second], here.left),
        (q.at[0, second], q.at[3, second], here.right),
        (q.at[0, first], q.at[1, first], here.left),
        (q.at[3, first], q.at[2, first], here.right),
        (q.at[1, second], q.at[2, second], here.left),
    )
    return [remote(s, t, send.at[k], recv.at[k], to) for k, (s, t, to) in enumerate(plan)]


LINEAR = -(5.0 / 16.0 + 3125.0 / 4096.0)
SQUARE = 3125.0 / 4096.0
CUBE = -1250.0 / 4096.0


def dot(left, right, dims=((1,), (0,))):
    return lax.dot_general(left, right, (dims, ((), ())), preferred_element_type=jnp.float32)


def column_parts(order, body):
    width = min(256, order)

    def one(part):
        body(pl.ds(pl.multiple_of(part * width, width), width))

    loop(order // width, one)


def excess(gram, result, first_b, second, second_b, third_b, tail_b, out):
    order = result.shape[0]

    def blend(columns):
        result[:, columns] = BETA * result[:, columns] + (1.0 - BETA) * gram(columns)

    column_parts(order, blend)
    whole = result[...]
    scale = 1.0 / jnp.sqrt(jnp.sum(whole * whole) + 1e-06)
    first_b[...] = (result[...] * scale).astype(jnp.bfloat16)

    def square(columns):
        value = dot(first_b[...], first_b[:, columns])
        second[:, columns] = value
        second_b[:, columns] = value.astype(jnp.bfloat16)

    column_parts(order, square)

    def cube(columns):
        third = dot(second_b[...], first_b[:, columns])
        first = result[:, columns] * scale
        two = second[:, columns]
        third_b[:, columns] = third.astype(jnp.bfloat16)
        tail_b[:, columns] = ((250.0 * first - 25.0 * two + third) * (1.0 / 4096.0)).astype(jnp.bfloat16)
        second[:, columns] = LINEAR * first + SQUARE * two + CUBE * third

    column_parts(order, cube)

    def last(columns):
        out[:, columns] = (second[:, columns] + dot(tail_b[...], third_b[:, columns])).astype(jnp.bfloat16)

    column_parts(order, last)


def attend(query, key, value, out):
    length, width = query.shape
    scores = dot(query[...], key[...], ((1,), (1,))) * (1.0 / math.sqrt(width))
    causal = lax.broadcasted_iota(jnp.int32, (length, length), 0) >= lax.broadcasted_iota(
        jnp.int32, (length, length), 1
    )
    scores = jnp.where(causal, scores, -jnp.inf)
    weights = jnp.exp(scores - jnp.max(scores, axis=-1, keepdims=True))
    probs = (weights / jnp.sum(weights, axis=-1, keepdims=True)).astype(jnp.bfloat16)
    out[...] = dot(probs, value[...]).astype(jnp.bfloat16)


def step_kernel(
    cap, count, table, query, key, value, grads_hbm, left_hbm, right_hbm,
    left_next, right_next, update_ref, attended,
    *scratch,
):
    buffers = [scratch[5 * chunk : 5 * chunk + 5] for chunk in range(CHUNKS)]
    rest = scratch[5 * CHUNKS :]
    out_slabs, in_slabs, out_back, in_back = rest[0:4], rest[4:6], rest[6:8], rest[8:12]
    grads_ref, stat_left, stat_right = rest[12:15]
    q, block, first_b, second, second_b, third_b, tail_b, left_b, right_b, half_b = rest[15:25]
    x_send, x_recv, g_send, g_recv, a_send, a_recv, b_send, b_recv, load, store = rest[25:]
    here = Place(count)
    pairs = here.pairs
    total = CHUNKS * cap
    first, last = halves(cap)

    loads = [
        pltpu.make_async_copy(source, target, load.at[k])
        for k, (source, target) in enumerate(
            ((grads_hbm, grads_ref), (left_hbm, stat_left), (right_hbm, stat_right))
        )
    ]
    for copy in loads:
        copy.start()
    greet(here)
    loads[0].wait()

    def pack(chunk, relative, part):
        base = lax.rem(here.replica + relative, 4) * total + chunk * cap + part.start
        xs = buffers[chunk][0]

        def one(index):
            number = table[0, base + index]
            xs[relative, part.start + index] = to_slab(grads_ref[number].astype(jnp.float32)).astype(jnp.bfloat16)

        loop(part.size, one, unroll=4)

    def add(chunk, relative, arrived, part):
        xs = buffers[chunk][0]

        def one(index):
            at = part.start + index
            both = xs[relative, at].astype(jnp.float32) + arrived[at].astype(jnp.float32)
            xs[relative, at] = both.astype(jnp.bfloat16)

        loop(part.size, one, unroll=4)

    reduce = [
        scatter_copies(here, cap, buffers[chunk], x_send.at[chunk], x_recv.at[chunk]) for chunk in range(CHUNKS)
    ]
    gather = [
        gather_copies(here, cap, chunk * cap, q, g_send.at[chunk], g_recv.at[chunk]) for chunk in range(CHUNKS)
    ]

    def open_chunk(chunk):
        for relative, part, copy in ((2, first, 0), (2, last, 1), (1, last, 2), (3, first, 3)):
            pack(chunk, relative, part)
            reduce[chunk][copy].start()
        for relative, part in ((1, first), (3, last), (0, first), (0, last)):
            pack(chunk, relative, part)

    def relay(chunk):
        reduce[chunk][0].wait_recv()
        add(chunk, 1, buffers[chunk][1], first)
        reduce[chunk][4].start()
        reduce[chunk][1].wait_recv()
        add(chunk, 3, buffers[chunk][2], last)
        reduce[chunk][5].start()

    def finish(chunk):
        for copy in range(2, 6):
            reduce[chunk][copy].wait_recv()
        xs, _, _, fl, fr = buffers[chunk]

        def one(owner):
            place = table[1, here.replica * (CHUNKS * pairs) + chunk * pairs + owner]
            at = jnp.maximum(place, 0)
            whole = xs[0, at].astype(jnp.float32) + fl[at].astype(jnp.float32) + fr[at].astype(jnp.float32)
            out_slabs[chunk][owner] = jnp.where(place >= 0, whole, 0.0).astype(jnp.bfloat16)

        loop(pairs, one, unroll=4)
        slot = chunk // 2
        hand_out(here, chunk % 2, out_slabs[chunk], in_slabs[slot], a_send.at[slot], a_recv.at[slot])

    def stored(slot, side):
        source, target = ((stat_left, left_next), (stat_right, right_next))[side]
        return pltpu.make_async_copy(source.at[slot], target.at[slot], store.at[slot, side])

    def precondition(slot):
        wait_all(in_slabs[slot], a_recv.at[slot])

        def place(pair):
            upper = from_slab(in_slabs[slot][2 * pair].astype(jnp.float32))
            lower = from_slab(in_slabs[slot][2 * pair + 1].astype(jnp.float32))
            rows = pl.ds(pl.multiple_of(pair * 16, 16), 16)
            block[rows] = jnp.concatenate([upper, lower], axis=0).astype(jnp.bfloat16)

        loop(count // 2, place, unroll=2)
        order = block.shape[0]
        spare = (first_b, second, second_b, third_b, tail_b)
        excess(
            lambda columns: dot(block[...], block[columns], ((1,), (1,))), stat_left.at[slot], *spare, left_b
        )
        stored(slot, 0).start()
        excess(
            lambda columns: dot(block[...], block[:, columns], ((0,), (0,))), stat_right.at[slot], *spare, right_b
        )
        stored(slot, 1).start()

        def left_side(columns):
            part = (25.0 / 16.0) * block[:, columns].astype(jnp.float32) + dot(left_b[...], block[:, columns])
            second[:, columns] = part
            half_b[:, columns] = part.astype(jnp.bfloat16)

        column_parts(order, left_side)

        def right_side(columns):
            second[:, columns] = (25.0 / 16.0) * second[:, columns] + dot(half_b[...], right_b[:, columns])

        column_parts(order, right_side)
        raw = second[...]
        widened = block[...].astype(jnp.float32)
        mean_raw = jnp.sum(raw * raw) * (1.0 / raw.size)
        mean_block = jnp.sum(widened * widened) * (1.0 / raw.size)
        scale = jnp.sqrt((mean_block + 1e-06) / (mean_raw + 1e-06))

        def cut(owner):
            rows = pl.ds(pl.multiple_of(owner * 8, 8), 8)
            out_back[slot][owner] = to_slab(second[rows] * scale).astype(jnp.bfloat16)

        loop(count, cut, unroll=4)
        for core in range(2):

            @pl.when(here.core == core)
            def _():
                chunk = slot * 2 + core
                hand_back(here, out_back[slot], in_back[chunk], b_send.at[slot], b_recv.at[chunk])

    def open_gather(chunk):
        wait_all(in_back[chunk], b_recv.at[chunk])
        for part, starts in ((first, (0, 3)), (last, (1, 2))):

            def one(index):
                at = chunk * cap + part.start + index
                q[0, at] = in_back[chunk][table[2, at]]

            loop(part.size, one, unroll=4)
            for copy in starts:
                gather[chunk][copy].start()

    def forward(chunk):
        for arrived, onward in ((0, 4), (1, 5)):
            gather[chunk][arrived].wait_recv()
            gather[chunk][onward].start()

    open_chunk(0)
    attend(query, key, value, attended)
    for chunk in range(CHUNKS):
        relay(chunk)
        if chunk + 1 < CHUNKS:
            open_chunk(chunk + 1)
        finish(chunk)
    loads[1].wait()
    loads[2].wait()
    precondition(0)
    precondition(1)
    for chunk in range(CHUNKS):
        open_gather(chunk)
        forward(chunk)
    for chunk in range(CHUNKS):
        for copy in range(2, 6):
            gather[chunk][copy].wait_recv()

    def settle(number):
        place = table[3, number]
        slab = q[place // total, place % total]
        update_ref[number] = from_slab(slab.astype(jnp.float32)).astype(jnp.bfloat16)

    loop(update_ref.shape[0], settle, unroll=8)
    for chunk in range(CHUNKS):
        for copy in reduce[chunk] + gather[chunk]:
            copy.wait_send()
    for slot in range(2):
        wait_all(out_back[slot].at[pl.ds(0, count - 1)], a_send.at[slot])
        wait_all(out_back[slot].at[pl.ds(0, count - 1)], b_send.at[slot])
        for side in range(2):
            stored(slot, side).wait()


def step(grads, stat_left, stat_right, query, key, value, table, cap, count, number):
    blocks, rows, columns = grads.shape
    order = stat_left.shape[1]
    slab = (2 * rows, columns // 2)
    narrow = VMEM((order, order), jnp.bfloat16)
    wide = VMEM((order, order), jnp.float32)
    some = VMEM((count // 2,) + slab, jnp.bfloat16)
    every = VMEM((count,) + slab, jnp.bfloat16)
    dma = pltpu.SemaphoreType.DMA
    near, far = pl.BlockSpec(memory_space=VMEM), pl.BlockSpec(memory_space=pl.ANY)
    return pl.pallas_call(
        functools.partial(step_kernel, cap, count),
        out_shape=(
            jax.ShapeDtypeStruct(stat_left.shape, jnp.float32),
            jax.ShapeDtypeStruct(stat_right.shape, jnp.float32),
            jax.ShapeDtypeStruct(grads.shape, jnp.bfloat16),
            jax.ShapeDtypeStruct(query.shape, jnp.bfloat16),
        ),
        in_specs=[pl.BlockSpec(memory_space=SMEM), near, near, near, far, far, far],
        out_specs=[far, far, near, near],
        scratch_shapes=[
            *[
                VMEM(lead + slab, jnp.bfloat16)
                for chunk in range(CHUNKS)
                for lead in ((4, cap), (cap,), (cap,), (cap,), (cap,))
            ],
            *[some] * 4, *[every] * 2, *[every] * 2, *[some] * 4,
            VMEM(grads.shape, jnp.bfloat16), VMEM(stat_left.shape, jnp.float32), VMEM(stat_left.shape, jnp.float32),
            VMEM((4, CHUNKS * cap) + slab, jnp.bfloat16),
            narrow, narrow, wide, narrow, narrow, narrow, narrow, narrow, narrow,
            dma((CHUNKS, 6)), dma((CHUNKS, 6)), dma((CHUNKS, 6)), dma((CHUNKS, 6)),
            dma((2,)), dma((2,)), dma((2,)), dma((CHUNKS,)), dma((3,)), dma((2, 2)),
        ],
        compiler_params=pltpu.CompilerParams(
            collective_id=number, has_side_effects=True, vmem_limit_bytes=56 * 2**20
        ),
    )(table, query, key, value, grads, stat_left, stat_right)


def table_kernel(cap, count, assign_ref, table):
    blocks = assign_ref.shape[1]
    pairs = count // 2
    slots = 8 * count
    width = table.shape[1]
    here = lax.axis_index("dp")
    wide = lax.broadcast_in_dim(assign_ref[...], (width, blocks), (0, 1))
    slot = wide.T
    number = lax.broadcasted_iota(jnp.int32, (blocks, width), 0)
    lane = lax.broadcasted_iota(jnp.int32, (blocks, width), 1)
    inside = lane % pairs
    chunk = (lane // pairs) % CHUNKS
    replica = lane // (CHUNKS * pairs)
    listed = replica * (CHUNKS * pairs) + 4 * inside + 2 * (chunk % 2) + chunk // 2
    hit = jnp.where(slot == listed, 1.0, 0.0)
    taken = jnp.sum(hit, axis=0, keepdims=True)
    before = lax.broadcasted_iota(jnp.int32, (width, width), 0)
    after = lax.broadcasted_iota(jnp.int32, (width, width), 1)
    counts = jnp.where((before < after) & (before // pairs == after // pairs), 1.0, 0.0).astype(jnp.bfloat16)
    rank = dot(lax.broadcast_in_dim(taken, (8, width), (0, 1)).astype(jnp.bfloat16), counts)[0:1]
    own_rank = jnp.sum(hit * rank, axis=1, keepdims=True).astype(jnp.int32)
    own_chunk = 2 * (slot % 2) + (slot // 2) % 2
    own_replica = slot // (CHUNKS * pairs)
    packed = own_chunk * cap + own_rank
    place = own_replica * (CHUNKS * cap) + packed
    table[...] = jnp.zeros(table.shape, jnp.int32)
    table[0:1] = jnp.sum(jnp.where(place == lane, number, 0), axis=0, keepdims=True)
    table[1:2] = jnp.where(taken > 0.0, rank.astype(jnp.int32), -1)
    owner = (slot // 4) % pairs
    table[2:3] = jnp.sum(jnp.where(place == lane + here * (CHUNKS * cap), owner, 0), axis=0, keepdims=True)
    relative = (own_replica - here + 4) % 4
    found = relative * (CHUNKS * cap) + packed
    table[3:4, 0:blocks] = found.T[0:1]
    most = jnp.max(own_rank + 1)
    table[4:5] = jnp.full((1, width), most, jnp.int32)


def make_table(assign, cap, count):
    width = 8 * count
    return pl.pallas_call(
        functools.partial(table_kernel, cap, count),
        out_shape=jax.ShapeDtypeStruct((8, width), jnp.int32),
        in_specs=[pl.BlockSpec(memory_space=VMEM)],
        out_specs=pl.BlockSpec(memory_space=VMEM),
        compiler_params=pltpu.CompilerParams(vmem_limit_bytes=32 * 2**20),
    )(assign.reshape(1, -1))


def body(partial_grads, stat_left, stat_right, assign, query_vectors, key_vectors, value_vectors):
    count = lax.axis_size("mp")
    full = count // 2
    cap = 3 * full // 4
    arrays = (
        partial_grads[0], stat_left[0], stat_right[0], query_vectors, key_vectors, value_vectors,
    )
    table = make_table(assign, cap, count)
    left_next, right_next, update, attended = lax.cond(
        table[4, 0] <= cap,
        lambda: step(*arrays, table, cap, count, 0),
        lambda: step(*arrays, make_table(assign, full, count), full, count, 1),
    )
    return (left_next[None], right_next[None], update, attended)


def solution(mesh):
    placed = (
        P("dp", None, "mp", None),
        P("dp", "mp", None, None),
        P("dp", "mp", None, None),
        P(),
        P("dp", "mp"),
        P("dp", "mp"),
        P("dp", "mp"),
    )
    return jax.shard_map(
        body,
        mesh=mesh,
        in_specs=placed,
        out_specs=(
            P("dp", "mp", None, None),
            P("dp", "mp", None, None),
            P(None, "mp", None),
            P("dp", "mp"),
        ),
        check_vma=False,
    )
```

```python
import functools
import math

import jax
import jax.numpy as jnp
from jax import lax
from jax.experimental import pallas as pl
from jax.experimental.pallas import tpu as pltpu
from jax.sharding import PartitionSpec as P

BETA = 0.9
MESH = pl.DeviceIdType.MESH
VMEM = pltpu.VMEM
SMEM = pltpu.SMEM


def to_slab(rows):
    half = rows.shape[1] // 2
    return jnp.concatenate([rows[:, :half], rows[:, half:]], axis=0)


def from_slab(slab):
    half = slab.shape[0] // 2
    return jnp.concatenate([slab[:half], slab[half:]], axis=1)


def loop(count, body, unroll=1):
    def step(index, carry):
        body(index)
        return carry

    lax.fori_loop(0, count, step, 0, unroll=unroll)


class Place:
    def __init__(self, count):
        self.count = count
        self.pairs = count // 2
        self.deep, self.wide = (8, 4) if count == 64 else (count // 2, 1)
        self.replica = lax.axis_index("dp")
        self.me = lax.axis_index("mp")
        self.pair, self.core = self.me // 2, self.me % 2
        self.right = {"dp": lax.rem(self.replica + 1, 4)}
        self.left = {"dp": lax.rem(self.replica + 3, 4)}

    def visit(self, send, cores=(0, 1)):
        z, y = self.pair // self.wide, self.pair % self.wide
        rows = [y] + [lax.rem(y + step, self.wide) for step in range(1, self.wide)]

        def turn(step):
            away = self.deep // 2 + (1 - 2 * (step % 2)) * ((step + 1) // 2)
            base = lax.rem(z + away, self.deep) * self.wide
            for row in rows:
                for core in cores:
                    send(base + row, core)

        loop(self.deep - 1, turn)
        for row in rows[1:]:
            for core in cores:
                send(z * self.wide + row, core)


CHUNKS = 4
PARTS = 4


def halves(cap):
    return pl.ds(0, cap // 2), pl.ds(cap // 2, cap - cap // 2)


def remote(src, dst, send_sem, recv_sem, device):
    return pltpu.make_async_remote_copy(
        src_ref=src, dst_ref=dst, send_sem=send_sem, recv_sem=recv_sem, device_id=device, device_id_type=MESH
    )


def greet(here):
    barrier = pltpu.get_barrier_semaphore()
    for device in (here.left, here.right, {"mp": here.pair * 2 + 1 - here.core}):
        pl.semaphore_signal(barrier, inc=1, device_id=device, device_id_type=MESH)

    def signal(pair, core):
        pl.semaphore_signal(barrier, inc=1, device_id={"mp": pair * 2 + core}, device_id_type=MESH)

    here.visit(signal)


def hand_out(here, core, src, dst, send_sem, recv_sem):
    def send(pair, core):
        remote(src.at[pair], dst.at[here.me], send_sem, recv_sem, {"mp": pair * 2 + core}).start()

    @pl.when(here.core == core)
    def _():
        pltpu.make_async_copy(src.at[here.pair], dst.at[here.me], recv_sem).start()

    @pl.when(here.core != core)
    def _():
        send(here.pair, core)

    here.visit(send, (core,))


def hand_back(here, src, dst, send_sem, recv_sem):
    def send(pair, core):
        device = pair * 2 + core
        remote(src.at[device], dst.at[here.me], send_sem, recv_sem, {"mp": device}).start()

    pltpu.make_async_copy(src.at[here.me], dst.at[here.me], recv_sem).start()
    send(here.pair, 1 - here.core)
    here.visit(send)


def wait_all(ref, sem):
    pltpu.make_async_copy(ref, ref, sem).wait()


def scatter_copies(here, cap, buffers, send, recv):
    first, second = halves(cap)
    xs, tl, tr, fl, fr = buffers
    plan = (
        (xs.at[2, first], tl.at[first], here.right),
        (xs.at[2, second], tr.at[second], here.left),
        (xs.at[1, second], fl.at[second], here.right),
        (xs.at[3, first], fr.at[first], here.left),
        (xs.at[1, first], fl.at[first], here.right),
        (xs.at[3, second], fr.at[second], here.left),
    )
    return [remote(s, t, send.at[k], recv.at[k], to) for k, (s, t, to) in enumerate(plan)]


def gather_copies(here, cap, q, send, recv):
    first, second = halves(cap)
    plan = (
        (q.at[0, first], q.at[3, first], here.right),
        (q.at[0, second], q.at[1, second], here.left),
        (q.at[0, second], q.at[3, second], here.right),
        (q.at[0, first], q.at[1, first], here.left),
        (q.at[3, first], q.at[2, first], here.right),
        (q.at[1, second], q.at[2, second], here.left),
    )
    return [remote(s, t, send.at[k], recv.at[k], to) for k, (s, t, to) in enumerate(plan)]


LINEAR = -(5.0 / 16.0 + 3125.0 / 4096.0)
SQUARE = 3125.0 / 4096.0
CUBE = -1250.0 / 4096.0


def dot(left, right, dims=((1,), (0,))):
    return lax.dot_general(left, right, (dims, ((), ())), preferred_element_type=jnp.float32)


def column_parts(order, body):
    width = min(256, order)

    def one(part):
        body(pl.ds(pl.multiple_of(part * width, width), width))

    loop(order // width, one)


def excess(gram, result, first_b, second, second_b, third_b, tail_b, out):
    order = result.shape[0]

    def blend(columns):
        result[:, columns] = BETA * result[:, columns] + (1.0 - BETA) * gram(columns)

    column_parts(order, blend)
    whole = result[...]
    scale = 1.0 / jnp.sqrt(jnp.sum(whole * whole) + 1e-06)
    first_b[...] = (result[...] * scale).astype(jnp.bfloat16)

    def square(columns):
        value = dot(first_b[...], first_b[:, columns])
        second[:, columns] = value
        second_b[:, columns] = value.astype(jnp.bfloat16)

    column_parts(order, square)

    def cube(columns):
        third = dot(second_b[...], first_b[:, columns])
        first = result[:, columns] * scale
        two = second[:, columns]
        third_b[:, columns] = third.astype(jnp.bfloat16)
        tail_b[:, columns] = ((250.0 * first - 25.0 * two + third) * (1.0 / 4096.0)).astype(jnp.bfloat16)
        second[:, columns] = LINEAR * first + SQUARE * two + CUBE * third

    column_parts(order, cube)

    def last(columns):
        out[:, columns] = (second[:, columns] + dot(tail_b[...], third_b[:, columns])).astype(jnp.bfloat16)

    column_parts(order, last)


def attend(query, key, value, out):
    length, width = query.shape
    scores = dot(query[...], key[...], ((1,), (1,))) * (1.0 / math.sqrt(width))
    causal = lax.broadcasted_iota(jnp.int32, (length, length), 0) >= lax.broadcasted_iota(
        jnp.int32, (length, length), 1
    )
    scores = jnp.where(causal, scores, -jnp.inf)
    weights = jnp.exp(scores - jnp.max(scores, axis=-1, keepdims=True))
    probs = (weights / jnp.sum(weights, axis=-1, keepdims=True)).astype(jnp.bfloat16)
    out[...] = dot(probs, value[...]).astype(jnp.bfloat16)


def step_kernel(
    bounds, back_cap, count, table, query, key, value, grads_hbm, left_hbm, right_hbm,
    left_next, right_next, update_ref, attended,
    *scratch,
):
    buffers = [scratch[5 * chunk : 5 * chunk + 5] for chunk in range(CHUNKS)]
    rest = scratch[5 * CHUNKS :]
    out_slabs, in_slabs, out_back, in_back, q = rest[0:4], rest[4:6], rest[6:10], rest[10:14], rest[14:18]
    summed, grads_ref, stat_left, stat_right = rest[18:22]
    block, first_b, second, second_b, third_b, tail_b, left_b, right_b, half_b = rest[22:31]
    x_send, x_recv, g_send, g_recv, a_send, a_recv, b_send, b_recv, load, store = rest[31:]
    here = Place(count)
    pairs = here.pairs
    total = bounds[-1]
    begins = (0,) + bounds[:-1]
    caps = [end - begin for begin, end in zip(begins, bounds)]

    loads = [
        pltpu.make_async_copy(source, target, load.at[k])
        for k, (source, target) in enumerate(
            ((grads_hbm, grads_ref), (left_hbm, stat_left), (right_hbm, stat_right))
        )
    ]
    for copy in loads:
        copy.start()
    greet(here)
    loads[0].wait()

    def pack(chunk, relative, part):
        base = lax.rem(here.replica + relative, 4) * total + begins[chunk] + part.start
        xs = buffers[chunk][0]

        def one(index):
            number = table[0, base + index]
            xs[relative, part.start + index] = to_slab(grads_ref[number].astype(jnp.float32)).astype(jnp.bfloat16)

        loop(part.size, one, unroll=4)

    def add(chunk, relative, arrived, part):
        xs = buffers[chunk][0]

        def one(index):
            at = part.start + index
            both = xs[relative, at].astype(jnp.float32) + arrived[at].astype(jnp.float32)
            xs[relative, at] = both.astype(jnp.bfloat16)

        loop(part.size, one, unroll=4)

    reduce = [
        scatter_copies(here, caps[chunk], buffers[chunk], x_send.at[chunk], x_recv.at[chunk]) for chunk in range(CHUNKS)
    ]
    gather = [
        gather_copies(here, back_cap, q[part], g_send.at[part], g_recv.at[part]) for part in range(PARTS)
    ]

    def open_chunk(chunk):
        first, last = halves(caps[chunk])
        for relative, part, copy in ((2, first, 0), (2, last, 1), (1, last, 2), (3, first, 3)):
            pack(chunk, relative, part)
            if chunk > 0:
                reduce[chunk][copy].start()
        for relative, part in ((1, first), (3, last), (0, first), (0, last)):
            pack(chunk, relative, part)
        if chunk == 0:
            pl.semaphore_wait(pltpu.get_barrier_semaphore(), here.count + 1)
            for copy in range(4):
                reduce[chunk][copy].start()

    def relay(chunk):
        first, last = halves(caps[chunk])
        reduce[chunk][0].wait_recv()
        add(chunk, 1, buffers[chunk][1], first)
        reduce[chunk][4].start()
        reduce[chunk][1].wait_recv()
        add(chunk, 3, buffers[chunk][2], last)
        reduce[chunk][5].start()

    def finish(chunk):
        for copy in range(2, 6):
            reduce[chunk][copy].wait_recv()
        xs, _, _, fl, fr = buffers[chunk]

        def gather_up(index):
            whole = xs[0, index].astype(jnp.float32) + fl[index].astype(jnp.float32) + fr[index].astype(jnp.float32)
            summed[begins[chunk] + index] = whole.astype(jnp.bfloat16)

        loop(caps[chunk], gather_up, unroll=4)

        def one(owner):
            place = table[1, here.replica * (CHUNKS * pairs) + chunk * pairs + owner]
            whole = summed[jnp.maximum(place, 0)].astype(jnp.float32)
            out_slabs[chunk][owner] = jnp.where(place >= 0, whole, 0.0).astype(jnp.bfloat16)

        loop(pairs, one, unroll=4)
        slot = chunk // 2
        hand_out(here, chunk % 2, out_slabs[chunk], in_slabs[slot], a_send.at[slot], a_recv.at[slot])

    def stored(slot, side):
        source, target = ((stat_left, left_next), (stat_right, right_next))[side]
        return pltpu.make_async_copy(source.at[slot], target.at[slot], store.at[slot, side])

    spare = (first_b, second, second_b, third_b, tail_b)

    def left_root(slot):
        wait_all(in_slabs[slot], a_recv.at[slot])

        def place(pair):
            upper = from_slab(in_slabs[slot][2 * pair].astype(jnp.float32))
            lower = from_slab(in_slabs[slot][2 * pair + 1].astype(jnp.float32))
            rows = pl.ds(pl.multiple_of(pair * 16, 16), 16)
            block[rows] = jnp.concatenate([upper, lower], axis=0).astype(jnp.bfloat16)

        loop(count // 2, place, unroll=2)
        excess(
            lambda columns: dot(block[...], block[columns], ((1,), (1,))), stat_left.at[slot], *spare, left_b
        )
        stored(slot, 0).start()

    def right_root(slot):
        excess(
            lambda columns: dot(block[...], block[:, columns], ((0,), (0,))), stat_right.at[slot], *spare, right_b
        )
        stored(slot, 1).start()

    def precondition(slot):
        order = block.shape[0]

        def left_side(columns):
            part = (25.0 / 16.0) * block[:, columns].astype(jnp.float32) + dot(left_b[...], block[:, columns])
            second[:, columns] = part
            half_b[:, columns] = part.astype(jnp.bfloat16)

        column_parts(order, left_side)

        def right_side(columns):
            second[:, columns] = (25.0 / 16.0) * second[:, columns] + dot(half_b[...], right_b[:, columns])

        column_parts(order, right_side)
        raw = second[...]
        widened = block[...].astype(jnp.float32)
        mean_raw = jnp.sum(raw * raw) * (1.0 / raw.size)
        mean_block = jnp.sum(widened * widened) * (1.0 / raw.size)
        scale = jnp.sqrt((mean_block + 1e-06) / (mean_raw + 1e-06))

        def cut(owner):
            rows = pl.ds(pl.multiple_of(owner * 8, 8), 8)
            ready = to_slab(second[rows] * scale).astype(jnp.bfloat16)
            width = ready.shape[1] // 2
            out_back[2 * slot][owner] = ready[:, :width]
            out_back[2 * slot + 1][owner] = ready[:, width:]

        loop(count, cut, unroll=4)

    def send_back(part):
        hand_back(here, out_back[part], in_back[part], b_send.at[part], b_recv.at[part])

    def open_gather(part):
        wait_all(in_back[part], b_recv.at[part])
        base = part // 2 * back_cap
        for half, starts in zip(halves(back_cap), ((0, 3), (1, 2))):

            def one(index):
                at = half.start + index
                q[part][0, at] = in_back[part][table[2, base + at]]

            loop(half.size, one, unroll=4)
            for copy in starts:
                gather[part][copy].start()

    def forward(chunk):
        for arrived, onward in ((0, 4), (1, 5)):
            gather[chunk][arrived].wait_recv()
            gather[chunk][onward].start()

    open_chunk(0)
    attend(query, key, value, attended)
    for chunk in range(CHUNKS):
        relay(chunk)
        if chunk + 1 < CHUNKS:
            open_chunk(chunk + 1)
        else:
            loads[1].wait()
            loads[2].wait()
            left_root(0)
        finish(chunk)
    right_root(0)
    precondition(0)
    send_back(0)
    send_back(1)
    left_root(1)
    right_root(1)
    open_gather(0)
    precondition(1)
    send_back(2)
    forward(0)
    send_back(3)
    for part in range(1, PARTS):
        open_gather(part)
        forward(part)
    for part in range(PARTS):
        for copy in range(2, 6):
            gather[part][copy].wait_recv()

    def settle(number):
        place = table[3, number]
        slot, inside = place // (4 * back_cap), place % (4 * back_cap)
        relative, at = inside // back_cap, inside % back_cap
        pieces = [q[part][relative, at].astype(jnp.float32) for part in range(PARTS)]
        sides = [jnp.where(slot == 0, pieces[side], pieces[2 + side]) for side in range(2)]
        slab = jnp.concatenate(sides, axis=1)
        update_ref[number] = from_slab(slab).astype(jnp.bfloat16)

    loop(update_ref.shape[0], settle, unroll=8)
    for copies in reduce + gather:
        for copy in copies:
            copy.wait_send()
    for slot in range(2):
        wait_all(in_slabs[slot].at[pl.ds(0, count - 1)], a_send.at[slot])
        for side in range(2):
            stored(slot, side).wait()
    for part in range(PARTS):
        wait_all(out_back[part].at[pl.ds(0, count - 1)], b_send.at[part])


def step(grads, stat_left, stat_right, query, key, value, table, bounds, back_cap, count, number):
    blocks, rows, columns = grads.shape
    order = stat_left.shape[1]
    slab, thin = (2 * rows, columns // 2), (2 * rows, columns // 4)
    narrow = VMEM((order, order), jnp.bfloat16)
    wide = VMEM((order, order), jnp.float32)
    some = VMEM((count // 2,) + slab, jnp.bfloat16)
    every = VMEM((count,) + slab, jnp.bfloat16)
    slim = VMEM((count,) + thin, jnp.bfloat16)
    dma = pltpu.SemaphoreType.DMA
    near, far = pl.BlockSpec(memory_space=VMEM), pl.BlockSpec(memory_space=pl.ANY)
    return pl.pallas_call(
        functools.partial(step_kernel, bounds, back_cap, count),
        out_shape=(
            jax.ShapeDtypeStruct(stat_left.shape, jnp.float32),
            jax.ShapeDtypeStruct(stat_right.shape, jnp.float32),
            jax.ShapeDtypeStruct(grads.shape, jnp.bfloat16),
            jax.ShapeDtypeStruct(query.shape, jnp.bfloat16),
        ),
        in_specs=[pl.BlockSpec(memory_space=SMEM), near, near, near, far, far, far],
        out_specs=[far, far, near, near],
        scratch_shapes=[
            *[
                VMEM(lead + slab, jnp.bfloat16)
                for cap in [end - begin for begin, end in zip((0,) + bounds, bounds)]
                for lead in ((4, cap), (cap,), (cap,), (cap,), (cap,))
            ],
            *[some] * 4, *[every] * 2, *[slim] * (2 * PARTS),
            *[VMEM((4, back_cap) + thin, jnp.bfloat16)] * PARTS,
            VMEM((bounds[-1],) + slab, jnp.bfloat16),
            VMEM(grads.shape, jnp.bfloat16), VMEM(stat_left.shape, jnp.float32), VMEM(stat_left.shape, jnp.float32),
            narrow, narrow, wide, narrow, narrow, narrow, narrow, narrow, narrow,
            dma((CHUNKS, 6)), dma((CHUNKS, 6)), dma((PARTS, 6)), dma((PARTS, 6)),
            dma((2,)), dma((2,)), dma((PARTS,)), dma((PARTS,)), dma((3,)), dma((2, 2)),
        ],
        compiler_params=pltpu.CompilerParams(
            collective_id=number, has_side_effects=True, vmem_limit_bytes=56 * 2**20
        ),
    )(table, query, key, value, grads, stat_left, stat_right)


def table_kernel(bounds, back_cap, count, assign_ref, table, over):
    blocks = assign_ref.shape[1]
    pairs = count // 2
    slots = 8 * count
    width = table.shape[1]
    here = lax.axis_index("dp")
    wide = lax.broadcast_in_dim(assign_ref[...], (width, blocks), (0, 1))
    slot = wide.T
    number = lax.broadcasted_iota(jnp.int32, (blocks, width), 0)
    lane = lax.broadcasted_iota(jnp.int32, (blocks, width), 1)
    inside = lane % pairs
    chunk = (lane // pairs) % CHUNKS
    replica = lane // (CHUNKS * pairs)
    listed = replica * (CHUNKS * pairs) + 4 * inside + 2 * (chunk % 2) + chunk // 2
    hit = jnp.where(slot == listed, 1.0, 0.0)
    taken = jnp.sum(hit, axis=0, keepdims=True)
    before = lax.broadcasted_iota(jnp.int32, (width, width), 0)
    after = lax.broadcasted_iota(jnp.int32, (width, width), 1)
    taken_b = lax.broadcast_in_dim(taken, (8, width), (0, 1)).astype(jnp.bfloat16)

    def ranks(group):
        counts = jnp.where((before < after) & (before // group == after // group), 1.0, 0.0).astype(jnp.bfloat16)
        rank = dot(taken_b, counts)[0:1]
        return rank, jnp.sum(hit * rank, axis=1, keepdims=True).astype(jnp.int32)

    rank, own_rank = ranks(CHUNKS * pairs)
    _, back_rank = ranks(2 * pairs)
    own_chunk = 2 * (slot % 2) + (slot // 2) % 2
    own_replica = slot // (CHUNKS * pairs)
    place = own_replica * bounds[-1] + own_rank
    bound = jnp.full(own_chunk.shape, bounds[0], jnp.int32)
    for chunk_number in range(1, CHUNKS):
        bound = jnp.where(own_chunk == chunk_number, bounds[chunk_number], bound)
    table[...] = jnp.zeros(table.shape, jnp.int32)
    table[0:1] = jnp.sum(jnp.where(place == lane, number, 0), axis=0, keepdims=True)
    table[1:2] = jnp.where(taken > 0.0, rank.astype(jnp.int32), -1)
    owner = (slot // 2) % count
    back = (slot % 2) * back_cap + back_rank
    mine = jnp.where(own_replica == here, back, -1)
    table[2:3] = jnp.sum(jnp.where(mine == lane, owner, 0), axis=0, keepdims=True)
    relative = (own_replica - here + 4) % 4
    found = (slot % 2) * (4 * back_cap) + relative * back_cap + back_rank
    table[3:4, 0:blocks] = found.T[0:1]
    over[0, 0] = jnp.maximum(jnp.max(own_rank - bound), jnp.max(back_rank) - back_cap) + 1


def make_table(assign, bounds, back_cap, count):
    width = 8 * count
    return pl.pallas_call(
        functools.partial(table_kernel, bounds, back_cap, count),
        out_shape=(jax.ShapeDtypeStruct((8, width), jnp.int32), jax.ShapeDtypeStruct((1, 1), jnp.int32)),
        in_specs=[pl.BlockSpec(memory_space=VMEM)],
        out_specs=(pl.BlockSpec(memory_space=VMEM), pl.BlockSpec(memory_space=SMEM)),
        compiler_params=pltpu.CompilerParams(vmem_limit_bytes=32 * 2**20),
    )(assign.reshape(1, -1))


def body(partial_grads, stat_left, stat_right, assign, query_vectors, key_vectors, value_vectors):
    count = lax.axis_size("mp")
    arrays = (
        partial_grads[0], stat_left[0], stat_right[0], query_vectors, key_vectors, value_vectors,
    )
    pairs = count // 2
    tight = tuple(pairs * part // 4 for part in (3, 5, 7, 9)), 5 * count // 8
    full = tuple(pairs * part for part in (1, 2, 3, 4)), count
    table, over = make_table(assign, *tight, count)
    left_next, right_next, update, attended = lax.cond(
        over[0, 0] <= 0,
        lambda: step(*arrays, table, *tight, count, 0),
        lambda: step(*arrays, make_table(assign, *full, count)[0], *full, count, 1),
    )
    return (left_next[None], right_next[None], update, attended)


def solution(mesh):
    placed = (
        P("dp", None, "mp", None),
        P("dp", "mp", None, None),
        P("dp", "mp", None, None),
        P(),
        P("dp", "mp"),
        P("dp", "mp"),
        P("dp", "mp"),
    )
    return jax.shard_map(
        body,
        mesh=mesh,
        in_specs=placed,
        out_specs=(
            P("dp", "mp", None, None),
            P("dp", "mp", None, None),
            P(None, "mp", None),
            P("dp", "mp"),
        ),
        check_vma=False,
    )
```

```python
import functools
import math

import jax
import jax.numpy as jnp
from jax import lax
from jax.experimental import pallas as pl
from jax.experimental.pallas import tpu as pltpu
from jax.sharding import PartitionSpec as P

BETA = 0.9
MESH = pl.DeviceIdType.MESH
VMEM = pltpu.VMEM
SMEM = pltpu.SMEM


def to_slab(rows):
    half = rows.shape[1] // 2
    return jnp.concatenate([rows[:, :half], rows[:, half:]], axis=0)


def from_slab(slab):
    half = slab.shape[0] // 2
    return jnp.concatenate([slab[:half], slab[half:]], axis=1)


def loop(count, body, unroll=1):
    def step(index, carry):
        body(index)
        return carry

    lax.fori_loop(0, count, step, 0, unroll=unroll)


class Place:
    def __init__(self, count):
        self.count = count
        self.pairs = count // 2
        self.deep, self.wide = (8, 4) if count == 64 else (count // 2, 1)
        self.replica = lax.axis_index("dp")
        self.me = lax.axis_index("mp")
        self.pair, self.core = self.me // 2, self.me % 2
        self.right = {"dp": lax.rem(self.replica + 1, 4)}
        self.left = {"dp": lax.rem(self.replica + 3, 4)}

    def visit(self, send, cores=(0, 1)):
        z, y = self.pair // self.wide, self.pair % self.wide
        rows = [y] + [lax.rem(y + step, self.wide) for step in range(1, self.wide)]

        def turn(step):
            away = self.deep // 2 + (1 - 2 * (step % 2)) * ((step + 1) // 2)
            base = lax.rem(z + away, self.deep) * self.wide
            for row in rows:
                for core in cores:
                    send(base + row, core)

        loop(self.deep - 1, turn)
        for row in rows[1:]:
            for core in cores:
                send(z * self.wide + row, core)


CHUNKS = 4
PARTS = 4


def halves(cap):
    return pl.ds(0, cap // 2), pl.ds(cap // 2, cap - cap // 2)


def remote(src, dst, send_sem, recv_sem, device):
    return pltpu.make_async_remote_copy(
        src_ref=src, dst_ref=dst, send_sem=send_sem, recv_sem=recv_sem, device_id=device, device_id_type=MESH
    )


def greet(here):
    barrier = pltpu.get_barrier_semaphore()
    for device in (here.left, here.right, {"mp": here.pair * 2 + 1 - here.core}):
        pl.semaphore_signal(barrier, inc=1, device_id=device, device_id_type=MESH)

    def signal(pair, core):
        pl.semaphore_signal(barrier, inc=1, device_id={"mp": pair * 2 + core}, device_id_type=MESH)

    here.visit(signal)


def hand_out(here, core, src, dst, send_sem, recv_sem):
    def send(pair, core):
        remote(src.at[pair], dst.at[here.me], send_sem, recv_sem, {"mp": pair * 2 + core}).start()

    @pl.when(here.core == core)
    def _():
        pltpu.make_async_copy(src.at[here.pair], dst.at[here.me], recv_sem).start()

    @pl.when(here.core != core)
    def _():
        send(here.pair, core)

    here.visit(send, (core,))


def hand_back(here, src, dst, send_sem, recv_sem):
    def send(pair, core):
        device = pair * 2 + core
        remote(src.at[device], dst.at[here.me], send_sem, recv_sem, {"mp": device}).start()

    pltpu.make_async_copy(src.at[here.me], dst.at[here.me], recv_sem).start()
    send(here.pair, 1 - here.core)
    here.visit(send)


def wait_all(ref, sem):
    pltpu.make_async_copy(ref, ref, sem).wait()


def scatter_copies(here, cap, buffers, send, recv):
    first, second = halves(cap)
    xs, tl, tr, fl, fr = buffers
    plan = (
        (xs.at[2, first], tl.at[first], here.right),
        (xs.at[2, second], tr.at[second], here.left),
        (xs.at[1, second], fl.at[second], here.right),
        (xs.at[3, first], fr.at[first], here.left),
        (xs.at[1, first], fl.at[first], here.right),
        (xs.at[3, second], fr.at[second], here.left),
    )
    return [remote(s, t, send.at[k], recv.at[k], to) for k, (s, t, to) in enumerate(plan)]


def gather_copies(here, cap, q, send, recv):
    first, second = halves(cap)
    plan = (
        (q.at[0, first], q.at[3, first], here.right),
        (q.at[0, second], q.at[1, second], here.left),
        (q.at[0, second], q.at[3, second], here.right),
        (q.at[0, first], q.at[1, first], here.left),
        (q.at[3, first], q.at[2, first], here.right),
        (q.at[1, second], q.at[2, second], here.left),
    )
    return [remote(s, t, send.at[k], recv.at[k], to) for k, (s, t, to) in enumerate(plan)]


LINEAR = -(5.0 / 16.0 + 3125.0 / 4096.0)
SQUARE = 3125.0 / 4096.0
CUBE = -1250.0 / 4096.0


def dot(left, right, dims=((1,), (0,))):
    return lax.dot_general(left, right, (dims, ((), ())), preferred_element_type=jnp.float32)


def column_parts(order, body):
    width = min(256, order)
    for part in range(order // width):
        body(pl.ds(part * width, width))


def excess(gram, result, first_b, second, second_b, third_b, tail_b, out):
    order = result.shape[0]

    def blend(columns):
        result[:, columns] = BETA * result[:, columns] + (1.0 - BETA) * gram(columns)

    column_parts(order, blend)
    whole = result[...]
    scale = 1.0 / jnp.sqrt(jnp.sum(whole * whole) + 1e-06)
    first_b[...] = (result[...] * scale).astype(jnp.bfloat16)

    def square(columns):
        value = dot(first_b[...], first_b[:, columns])
        second[:, columns] = value
        second_b[:, columns] = value.astype(jnp.bfloat16)

    column_parts(order, square)

    def cube(columns):
        third = dot(second_b[...], first_b[:, columns])
        first = result[:, columns] * scale
        two = second[:, columns]
        third_b[:, columns] = third.astype(jnp.bfloat16)
        tail_b[:, columns] = ((250.0 * first - 25.0 * two + third) * (1.0 / 4096.0)).astype(jnp.bfloat16)
        second[:, columns] = LINEAR * first + SQUARE * two + CUBE * third

    column_parts(order, cube)

    def last(columns):
        out[:, columns] = (second[:, columns] + dot(tail_b[...], third_b[:, columns])).astype(jnp.bfloat16)

    column_parts(order, last)


def attend(query, key, value, out):
    length, width = query.shape
    scores = dot(query[...], key[...], ((1,), (1,))) * (1.0 / math.sqrt(width))
    causal = lax.broadcasted_iota(jnp.int32, (length, length), 0) >= lax.broadcasted_iota(
        jnp.int32, (length, length), 1
    )
    scores = jnp.where(causal, scores, -jnp.inf)
    weights = jnp.exp(scores - jnp.max(scores, axis=-1, keepdims=True))
    probs = (weights / jnp.sum(weights, axis=-1, keepdims=True)).astype(jnp.bfloat16)
    out[...] = dot(probs, value[...]).astype(jnp.bfloat16)


def step_kernel(
    bounds, back_cap, count, table, query, key, value, grads_hbm, left_hbm, right_hbm,
    left_next, right_next, update_ref, attended,
    *scratch,
):
    buffers = [scratch[5 * chunk : 5 * chunk + 5] for chunk in range(CHUNKS)]
    rest = scratch[5 * CHUNKS :]
    out_slabs, in_slabs, out_back, in_back, q = rest[0:4], rest[4:6], rest[6:10], rest[10:14], rest[14:18]
    summed, grads_ref, stat_left, stat_right = rest[18:22]
    block, first_b, second, second_b, third_b, tail_b, left_b, right_b, half_b = rest[22:31]
    x_send, x_recv, g_send, g_recv, a_send, a_recv, b_send, b_recv, load, store = rest[31:]
    here = Place(count)
    pairs = here.pairs
    total = bounds[-1]
    begins = (0,) + bounds[:-1]
    caps = [end - begin for begin, end in zip(begins, bounds)]

    loads = [
        pltpu.make_async_copy(source, target, load.at[k])
        for k, (source, target) in enumerate(
            ((grads_hbm, grads_ref), (left_hbm, stat_left), (right_hbm, stat_right))
        )
    ]
    for copy in loads:
        copy.start()
    greet(here)
    loads[0].wait()

    def pack(chunk, relative, part):
        base = lax.rem(here.replica + relative, 4) * total + begins[chunk] + part.start
        xs = buffers[chunk][0]

        def one(index):
            number = table[0, base + index]
            xs[relative, part.start + index] = to_slab(grads_ref[number].astype(jnp.float32)).astype(jnp.bfloat16)

        loop(part.size, one, unroll=4)

    def add(chunk, relative, arrived, part):
        xs = buffers[chunk][0]

        def one(index):
            at = part.start + index
            both = xs[relative, at].astype(jnp.float32) + arrived[at].astype(jnp.float32)
            xs[relative, at] = both.astype(jnp.bfloat16)

        loop(part.size, one, unroll=4)

    reduce = [
        scatter_copies(here, caps[chunk], buffers[chunk], x_send.at[chunk], x_recv.at[chunk]) for chunk in range(CHUNKS)
    ]
    gather = [
        gather_copies(here, back_cap, q[part], g_send.at[part], g_recv.at[part]) for part in range(PARTS)
    ]

    def open_chunk(chunk):
        first, last = halves(caps[chunk])
        for relative, part, copy in ((2, first, 0), (2, last, 1), (1, last, 2), (3, first, 3)):
            pack(chunk, relative, part)
            if chunk > 0:
                reduce[chunk][copy].start()
        for relative, part in ((1, first), (3, last), (0, first), (0, last)):
            pack(chunk, relative, part)
        if chunk == 0:
            pl.semaphore_wait(pltpu.get_barrier_semaphore(), here.count + 1)
            for copy in range(4):
                reduce[chunk][copy].start()

    def relay(chunk):
        first, last = halves(caps[chunk])
        reduce[chunk][0].wait_recv()
        add(chunk, 1, buffers[chunk][1], first)
        reduce[chunk][4].start()
        reduce[chunk][1].wait_recv()
        add(chunk, 3, buffers[chunk][2], last)
        reduce[chunk][5].start()

    def finish(chunk):
        for copy in range(2, 6):
            reduce[chunk][copy].wait_recv()
        xs, _, _, fl, fr = buffers[chunk]

        def gather_up(index):
            whole = xs[0, index].astype(jnp.float32) + fl[index].astype(jnp.float32) + fr[index].astype(jnp.float32)
            summed[begins[chunk] + index] = whole.astype(jnp.bfloat16)

        loop(caps[chunk], gather_up, unroll=4)

        def one(owner):
            place = table[1, here.replica * (CHUNKS * pairs) + chunk * pairs + owner]
            whole = summed[jnp.maximum(place, 0)].astype(jnp.float32)
            out_slabs[chunk][owner] = jnp.where(place >= 0, whole, 0.0).astype(jnp.bfloat16)

        loop(pairs, one, unroll=4)
        slot = chunk // 2
        hand_out(here, chunk % 2, out_slabs[chunk], in_slabs[slot], a_send.at[slot], a_recv.at[slot])

    def stored(slot, side):
        source, target = ((stat_left, left_next), (stat_right, right_next))[side]
        return pltpu.make_async_copy(source.at[slot], target.at[slot], store.at[slot, side])

    spare = (first_b, second, second_b, third_b, tail_b)

    def left_root(slot):
        wait_all(in_slabs[slot], a_recv.at[slot])

        def place(pair):
            upper = from_slab(in_slabs[slot][2 * pair].astype(jnp.float32))
            lower = from_slab(in_slabs[slot][2 * pair + 1].astype(jnp.float32))
            rows = pl.ds(pl.multiple_of(pair * 16, 16), 16)
            block[rows] = jnp.concatenate([upper, lower], axis=0).astype(jnp.bfloat16)

        loop(count // 2, place, unroll=2)
        excess(
            lambda columns: dot(block[...], block[columns], ((1,), (1,))), stat_left.at[slot], *spare, left_b
        )
        stored(slot, 0).start()

    def right_root(slot):
        excess(
            lambda columns: dot(block[...], block[:, columns], ((0,), (0,))), stat_right.at[slot], *spare, right_b
        )
        stored(slot, 1).start()

    def precondition(slot):
        order = block.shape[0]

        def left_side(columns):
            part = (25.0 / 16.0) * block[:, columns].astype(jnp.float32) + dot(left_b[...], block[:, columns])
            second[:, columns] = part
            half_b[:, columns] = part.astype(jnp.bfloat16)

        column_parts(order, left_side)

        def right_side(columns):
            second[:, columns] = (25.0 / 16.0) * second[:, columns] + dot(half_b[...], right_b[:, columns])

        column_parts(order, right_side)
        raw = second[...]
        widened = block[...].astype(jnp.float32)
        mean_raw = jnp.sum(raw * raw) * (1.0 / raw.size)
        mean_block = jnp.sum(widened * widened) * (1.0 / raw.size)
        scale = jnp.sqrt((mean_block + 1e-06) / (mean_raw + 1e-06))

        def cut(owner):
            rows = pl.ds(pl.multiple_of(owner * 8, 8), 8)
            ready = to_slab(second[rows] * scale).astype(jnp.bfloat16)
            width = ready.shape[1] // 2
            out_back[2 * slot][owner] = ready[:, :width]
            out_back[2 * slot + 1][owner] = ready[:, width:]

        loop(count, cut, unroll=4)

    def send_back(part):
        hand_back(here, out_back[part], in_back[part], b_send.at[part], b_recv.at[part])

    def sent_back(part):
        wait_all(out_back[part].at[pl.ds(0, count - 1)], b_send.at[part])

    def open_gather(part):
        wait_all(in_back[part], b_recv.at[part])
        base = part // 2 * back_cap
        for half, starts in zip(halves(back_cap), ((0, 3), (1, 2))):

            def one(index):
                at = half.start + index
                q[part][0, at] = in_back[part][table[2, base + at]]

            loop(half.size, one, unroll=4)
            for copy in starts:
                gather[part][copy].start()

    def forward(chunk):
        for arrived, onward in ((0, 4), (1, 5)):
            gather[chunk][arrived].wait_recv()
            gather[chunk][onward].start()

    open_chunk(0)
    attend(query, key, value, attended)
    for chunk in range(CHUNKS):
        relay(chunk)
        if chunk + 1 < CHUNKS:
            open_chunk(chunk + 1)
        else:
            loads[1].wait()
            loads[2].wait()
            left_root(0)
        finish(chunk)
    right_root(0)
    precondition(0)
    send_back(0)
    left_root(1)
    sent_back(0)
    send_back(1)
    right_root(1)
    open_gather(0)
    precondition(1)
    sent_back(1)
    send_back(2)
    forward(0)
    open_gather(1)
    sent_back(2)
    send_back(3)
    forward(1)
    for part in (2, 3):
        open_gather(part)
        forward(part)
    for part in range(PARTS):
        for copy in range(2, 6):
            gather[part][copy].wait_recv()

    def settle(number):
        place = table[3, number]
        slot, inside = place // (4 * back_cap), place % (4 * back_cap)
        relative, at = inside // back_cap, inside % back_cap
        pieces = [q[part][relative, at].astype(jnp.float32) for part in range(PARTS)]
        sides = [jnp.where(slot == 0, pieces[side], pieces[2 + side]) for side in range(2)]
        slab = jnp.concatenate(sides, axis=1)
        update_ref[number] = from_slab(slab).astype(jnp.bfloat16)

    loop(update_ref.shape[0], settle, unroll=8)
    for copies in reduce + gather:
        for copy in copies:
            copy.wait_send()
    for slot in range(2):
        wait_all(in_slabs[slot].at[pl.ds(0, count - 1)], a_send.at[slot])
        for side in range(2):
            stored(slot, side).wait()
    sent_back(3)


def step(grads, stat_left, stat_right, query, key, value, table, bounds, back_cap, count, number):
    blocks, rows, columns = grads.shape
    order = stat_left.shape[1]
    slab, thin = (2 * rows, columns // 2), (2 * rows, columns // 4)
    narrow = VMEM((order, order), jnp.bfloat16)
    wide = VMEM((order, order), jnp.float32)
    some = VMEM((count // 2,) + slab, jnp.bfloat16)
    every = VMEM((count,) + slab, jnp.bfloat16)
    slim = VMEM((count,) + thin, jnp.bfloat16)
    dma = pltpu.SemaphoreType.DMA
    near, far = pl.BlockSpec(memory_space=VMEM), pl.BlockSpec(memory_space=pl.ANY)
    return pl.pallas_call(
        functools.partial(step_kernel, bounds, back_cap, count),
        out_shape=(
            jax.ShapeDtypeStruct(stat_left.shape, jnp.float32),
            jax.ShapeDtypeStruct(stat_right.shape, jnp.float32),
            jax.ShapeDtypeStruct(grads.shape, jnp.bfloat16),
            jax.ShapeDtypeStruct(query.shape, jnp.bfloat16),
        ),
        in_specs=[pl.BlockSpec(memory_space=SMEM), near, near, near, far, far, far],
        out_specs=[far, far, near, near],
        scratch_shapes=[
            *[
                VMEM(lead + slab, jnp.bfloat16)
                for cap in [end - begin for begin, end in zip((0,) + bounds, bounds)]
                for lead in ((4, cap), (cap,), (cap,), (cap,), (cap,))
            ],
            *[some] * 4, *[every] * 2, *[slim] * (2 * PARTS),
            *[VMEM((4, back_cap) + thin, jnp.bfloat16)] * PARTS,
            VMEM((bounds[-1],) + slab, jnp.bfloat16),
            VMEM(grads.shape, jnp.bfloat16), VMEM(stat_left.shape, jnp.float32), VMEM(stat_left.shape, jnp.float32),
            narrow, narrow, wide, narrow, narrow, narrow, narrow, narrow, narrow,
            dma((CHUNKS, 6)), dma((CHUNKS, 6)), dma((PARTS, 6)), dma((PARTS, 6)),
            dma((2,)), dma((2,)), dma((PARTS,)), dma((PARTS,)), dma((3,)), dma((2, 2)),
        ],
        compiler_params=pltpu.CompilerParams(
            collective_id=number, has_side_effects=True, vmem_limit_bytes=56 * 2**20
        ),
    )(table, query, key, value, grads, stat_left, stat_right)


def table_kernel(bounds, back_cap, count, assign_ref, table, over):
    blocks = assign_ref.shape[1]
    pairs = count // 2
    slots = 8 * count
    width = table.shape[1]
    here = lax.axis_index("dp")
    wide = lax.broadcast_in_dim(assign_ref[...], (width, blocks), (0, 1))
    slot = wide.T
    number = lax.broadcasted_iota(jnp.int32, (blocks, width), 0)
    lane = lax.broadcasted_iota(jnp.int32, (blocks, width), 1)
    inside = lane % pairs
    chunk = (lane // pairs) % CHUNKS
    replica = lane // (CHUNKS * pairs)
    listed = replica * (CHUNKS * pairs) + 4 * inside + 2 * (chunk % 2) + chunk // 2
    hit = jnp.where(slot == listed, 1.0, 0.0)
    taken = jnp.sum(hit, axis=0, keepdims=True)
    before = lax.broadcasted_iota(jnp.int32, (width, width), 0)
    after = lax.broadcasted_iota(jnp.int32, (width, width), 1)
    taken_b = lax.broadcast_in_dim(taken, (8, width), (0, 1)).astype(jnp.bfloat16)

    def ranks(group):
        counts = jnp.where((before < after) & (before // group == after // group), 1.0, 0.0).astype(jnp.bfloat16)
        rank = dot(taken_b, counts)[0:1]
        return rank, jnp.sum(hit * rank, axis=1, keepdims=True).astype(jnp.int32)

    rank, own_rank = ranks(CHUNKS * pairs)
    _, back_rank = ranks(2 * pairs)
    own_chunk = 2 * (slot % 2) + (slot // 2) % 2
    own_replica = slot // (CHUNKS * pairs)
    place = own_replica * bounds[-1] + own_rank
    bound = jnp.full(own_chunk.shape, bounds[0], jnp.int32)
    for chunk_number in range(1, CHUNKS):
        bound = jnp.where(own_chunk == chunk_number, bounds[chunk_number], bound)
    table[...] = jnp.zeros(table.shape, jnp.int32)
    table[0:1] = jnp.sum(jnp.where(place == lane, number, 0), axis=0, keepdims=True)
    table[1:2] = jnp.where(taken > 0.0, rank.astype(jnp.int32), -1)
    owner = (slot // 2) % count
    back = (slot % 2) * back_cap + back_rank
    mine = jnp.where(own_replica == here, back, -1)
    table[2:3] = jnp.sum(jnp.where(mine == lane, owner, 0), axis=0, keepdims=True)
    relative = (own_replica - here + 4) % 4
    found = (slot % 2) * (4 * back_cap) + relative * back_cap + back_rank
    table[3:4, 0:blocks] = found.T[0:1]
    over[0, 0] = jnp.maximum(jnp.max(own_rank - bound), jnp.max(back_rank) - back_cap) + 1


def make_table(assign, bounds, back_cap, count):
    width = 8 * count
    return pl.pallas_call(
        functools.partial(table_kernel, bounds, back_cap, count),
        out_shape=(jax.ShapeDtypeStruct((8, width), jnp.int32), jax.ShapeDtypeStruct((1, 1), jnp.int32)),
        in_specs=[pl.BlockSpec(memory_space=VMEM)],
        out_specs=(pl.BlockSpec(memory_space=VMEM), pl.BlockSpec(memory_space=SMEM)),
        compiler_params=pltpu.CompilerParams(vmem_limit_bytes=32 * 2**20),
    )(assign.reshape(1, -1))


def body(partial_grads, stat_left, stat_right, assign, query_vectors, key_vectors, value_vectors):
    count = lax.axis_size("mp")
    arrays = (
        partial_grads[0], stat_left[0], stat_right[0], query_vectors, key_vectors, value_vectors,
    )
    pairs = count // 2
    tight = tuple(pairs * part // 4 for part in (3, 5, 7, 9)), 5 * count // 8
    full = tuple(pairs * part for part in (1, 2, 3, 4)), count
    table, over = make_table(assign, *tight, count)
    left_next, right_next, update, attended = lax.cond(
        over[0, 0] <= 0,
        lambda: step(*arrays, table, *tight, count, 0),
        lambda: step(*arrays, make_table(assign, *full, count)[0], *full, count, 1),
    )
    return (left_next[None], right_next[None], update, attended)


def solution(mesh):
    placed = (
        P("dp", None, "mp", None),
        P("dp", "mp", None, None),
        P("dp", "mp", None, None),
        P(),
        P("dp", "mp"),
        P("dp", "mp"),
        P("dp", "mp"),
    )
    return jax.shard_map(
        body,
        mesh=mesh,
        in_specs=placed,
        out_specs=(
            P("dp", "mp", None, None),
            P("dp", "mp", None, None),
            P(None, "mp", None),
            P("dp", "mp"),
        ),
        check_vma=False,
    )
```

```python
import functools
import math

import jax
import jax.numpy as jnp
from jax import lax
from jax.experimental import pallas as pl
from jax.experimental.pallas import tpu as pltpu
from jax.sharding import PartitionSpec as P

BETA = 0.9
MESH = pl.DeviceIdType.MESH
VMEM = pltpu.VMEM
SMEM = pltpu.SMEM


def to_slab(rows):
    half = rows.shape[1] // 2
    return jnp.concatenate([rows[:, :half], rows[:, half:]], axis=0)


def from_slab(slab):
    half = slab.shape[0] // 2
    return jnp.concatenate([slab[:half], slab[half:]], axis=1)


def loop(count, body, unroll=1):
    def step(index, carry):
        body(index)
        return carry

    lax.fori_loop(0, count, step, 0, unroll=unroll)


class Place:
    def __init__(self, count):
        self.count = count
        self.pairs = count // 2
        self.deep, self.wide = (8, 4) if count == 64 else (count // 2, 1)
        self.replica = lax.axis_index("dp")
        self.me = lax.axis_index("mp")
        self.pair, self.core = self.me // 2, self.me % 2
        self.right = {"dp": lax.rem(self.replica + 1, 4)}
        self.left = {"dp": lax.rem(self.replica + 3, 4)}

    def visit(self, send, cores=(0, 1)):
        z, y = self.pair // self.wide, self.pair % self.wide
        rows = [y] + [lax.rem(y + step, self.wide) for step in range(1, self.wide)]

        def turn(step):
            away = self.deep // 2 + (1 - 2 * (step % 2)) * ((step + 1) // 2)
            base = lax.rem(z + away, self.deep) * self.wide
            for row in rows:
                for core in cores:
                    send(base + row, core)

        loop(self.deep - 1, turn)
        for row in rows[1:]:
            for core in cores:
                send(z * self.wide + row, core)


CHUNKS = 4
PARTS = 4


def halves(cap):
    return pl.ds(0, cap // 2), pl.ds(cap // 2, cap - cap // 2)


def remote(src, dst, send_sem, recv_sem, device):
    return pltpu.make_async_remote_copy(
        src_ref=src, dst_ref=dst, send_sem=send_sem, recv_sem=recv_sem, device_id=device, device_id_type=MESH
    )


def greet(here):
    barrier = pltpu.get_barrier_semaphore()
    for device in (here.left, here.right, {"mp": here.pair * 2 + 1 - here.core}):
        pl.semaphore_signal(barrier, inc=1, device_id=device, device_id_type=MESH)

    def signal(pair, core):
        pl.semaphore_signal(barrier, inc=1, device_id={"mp": pair * 2 + core}, device_id_type=MESH)

    here.visit(signal)


def hand_out(here, core, src, dst, send_sem, recv_sem):
    def send(pair, core):
        remote(src.at[pair], dst.at[here.me], send_sem, recv_sem, {"mp": pair * 2 + core}).start()

    @pl.when(here.core == core)
    def _():
        pltpu.make_async_copy(src.at[here.pair], dst.at[here.me], recv_sem).start()

    @pl.when(here.core != core)
    def _():
        send(here.pair, core)

    here.visit(send, (core,))


def hand_back(here, src, dst, send_sem, recv_sem):
    def send(pair, core):
        device = pair * 2 + core
        remote(src.at[device], dst.at[here.me], send_sem, recv_sem, {"mp": device}).start()

    pltpu.make_async_copy(src.at[here.me], dst.at[here.me], recv_sem).start()
    send(here.pair, 1 - here.core)
    here.visit(send)


def wait_all(ref, sem):
    pltpu.make_async_copy(ref, ref, sem).wait()


def scatter_copies(here, cap, buffers, send, recv):
    first, second = halves(cap)
    xs, tl, tr, fl, fr = buffers
    plan = (
        (xs.at[2, first], tl.at[first], here.right),
        (xs.at[2, second], tr.at[second], here.left),
        (xs.at[1, second], fl.at[second], here.right),
        (xs.at[3, first], fr.at[first], here.left),
        (xs.at[1, first], fl.at[first], here.right),
        (xs.at[3, second], fr.at[second], here.left),
    )
    return [remote(s, t, send.at[k], recv.at[k], to) for k, (s, t, to) in enumerate(plan)]


def gather_copies(here, cap, q, send, recv):
    first, second = halves(cap)
    plan = (
        (q.at[0, first], q.at[3, first], here.right),
        (q.at[0, second], q.at[1, second], here.left),
        (q.at[0, second], q.at[3, second], here.right),
        (q.at[0, first], q.at[1, first], here.left),
        (q.at[3, first], q.at[2, first], here.right),
        (q.at[1, second], q.at[2, second], here.left),
    )
    return [remote(s, t, send.at[k], recv.at[k], to) for k, (s, t, to) in enumerate(plan)]


LINEAR = -(5.0 / 16.0 + 3125.0 / 4096.0)
SQUARE = 3125.0 / 4096.0
CUBE = -1250.0 / 4096.0


def dot(left, right, dims=((1,), (0,))):
    return lax.dot_general(left, right, (dims, ((), ())), preferred_element_type=jnp.float32)


def column_parts(order, body):
    width = min(256, order)
    for part in range(order // width):
        body(pl.ds(part * width, width))


def excess(gram, result, first_b, second, second_b, third_b, tail_b, out):
    order = result.shape[0]

    def blend(columns):
        result[:, columns] = BETA * result[:, columns] + (1.0 - BETA) * gram(columns)

    column_parts(order, blend)
    whole = result[...]
    scale = 1.0 / jnp.sqrt(jnp.sum(whole * whole) + 1e-06)
    first_b[...] = (result[...] * scale).astype(jnp.bfloat16)

    def square(columns):
        value = dot(first_b[...], first_b[:, columns])
        second[:, columns] = value
        second_b[:, columns] = value.astype(jnp.bfloat16)

    column_parts(order, square)

    def cube(columns):
        third = dot(second_b[...], first_b[:, columns])
        first = result[:, columns] * scale
        two = second[:, columns]
        third_b[:, columns] = third.astype(jnp.bfloat16)
        tail_b[:, columns] = ((250.0 * first - 25.0 * two + third) * (1.0 / 4096.0)).astype(jnp.bfloat16)
        second[:, columns] = LINEAR * first + SQUARE * two + CUBE * third

    column_parts(order, cube)

    def last(columns):
        out[:, columns] = (second[:, columns] + dot(tail_b[...], third_b[:, columns])).astype(jnp.bfloat16)

    column_parts(order, last)


def attend(query, key, value, out):
    length, width = query.shape
    scores = dot(query[...], key[...], ((1,), (1,))) * (1.0 / math.sqrt(width))
    causal = lax.broadcasted_iota(jnp.int32, (length, length), 0) >= lax.broadcasted_iota(
        jnp.int32, (length, length), 1
    )
    scores = jnp.where(causal, scores, -jnp.inf)
    weights = jnp.exp(scores - jnp.max(scores, axis=-1, keepdims=True))
    probs = (weights / jnp.sum(weights, axis=-1, keepdims=True)).astype(jnp.bfloat16)
    out[...] = dot(probs, value[...]).astype(jnp.bfloat16)


def step_kernel(
    bounds, back_cap, count, table, query, key, value, grads_hbm, left_hbm, right_hbm,
    left_next, right_next, update_ref, attended,
    *scratch,
):
    buffers = [scratch[5 * chunk : 5 * chunk + 5] for chunk in range(CHUNKS)]
    rest = scratch[5 * CHUNKS :]
    out_slabs, in_slabs, out_back, in_back, q = rest[0:4], rest[4:6], rest[6:10], rest[10:14], rest[14:18]
    summed, grads_ref, stat_left, stat_right = rest[18:22]
    block, first_b, second, second_b, third_b, tail_b, left_b, right_b, half_b = rest[22:31]
    x_send, x_recv, g_send, g_recv, a_send, a_recv, b_send, b_recv, load, store = rest[31:]
    here = Place(count)
    pairs = here.pairs
    total = bounds[-1]
    begins = (0,) + bounds[:-1]
    caps = [end - begin for begin, end in zip(begins, bounds)]

    loads = [
        pltpu.make_async_copy(source, target, load.at[k])
        for k, (source, target) in enumerate(
            ((grads_hbm, grads_ref), (left_hbm, stat_left), (right_hbm, stat_right))
        )
    ]
    for copy in loads:
        copy.start()
    greet(here)
    loads[0].wait()

    def pack(chunk, relative, part):
        base = lax.rem(here.replica + relative, 4) * total + begins[chunk] + part.start
        xs = buffers[chunk][0]

        def one(index):
            number = table[0, base + index]
            xs[relative, part.start + index] = to_slab(grads_ref[number].astype(jnp.float32)).astype(jnp.bfloat16)

        loop(part.size, one, unroll=4)

    def add(chunk, relative, arrived, part):
        xs = buffers[chunk][0]

        def one(index):
            at = part.start + index
            both = xs[relative, at].astype(jnp.float32) + arrived[at].astype(jnp.float32)
            xs[relative, at] = both.astype(jnp.bfloat16)

        loop(part.size, one, unroll=4)

    reduce = [
        scatter_copies(here, caps[chunk], buffers[chunk], x_send.at[chunk], x_recv.at[chunk]) for chunk in range(CHUNKS)
    ]
    gather = [
        gather_copies(here, back_cap, q[part], g_send.at[part], g_recv.at[part]) for part in range(PARTS)
    ]

    def open_chunk(chunk):
        first, last = halves(caps[chunk])
        for relative, part, copy in ((2, first, 0), (2, last, 1), (1, last, 2), (3, first, 3)):
            pack(chunk, relative, part)
            if chunk > 0:
                reduce[chunk][copy].start()
        for relative, part in ((1, first), (3, last), (0, first), (0, last)):
            pack(chunk, relative, part)
        if chunk == 0:
            pl.semaphore_wait(pltpu.get_barrier_semaphore(), here.count + 1)
            for copy in range(4):
                reduce[chunk][copy].start()

    def relay(chunk):
        first, last = halves(caps[chunk])
        reduce[chunk][0].wait_recv()
        add(chunk, 1, buffers[chunk][1], first)
        reduce[chunk][4].start()
        reduce[chunk][1].wait_recv()
        add(chunk, 3, buffers[chunk][2], last)
        reduce[chunk][5].start()

    def finish(chunk):
        for copy in range(2, 6):
            reduce[chunk][copy].wait_recv()
        xs, _, _, fl, fr = buffers[chunk]

        def gather_up(index):
            whole = xs[0, index].astype(jnp.float32) + fl[index].astype(jnp.float32) + fr[index].astype(jnp.float32)
            summed[begins[chunk] + index] = whole.astype(jnp.bfloat16)

        loop(caps[chunk], gather_up, unroll=4)

        def one(owner):
            place = table[1, here.replica * (CHUNKS * pairs) + chunk * pairs + owner]
            whole = summed[jnp.maximum(place, 0)].astype(jnp.float32)
            out_slabs[chunk][owner] = jnp.where(place >= 0, whole, 0.0).astype(jnp.bfloat16)

        loop(pairs, one, unroll=4)
        slot = chunk // 2
        hand_out(here, chunk % 2, out_slabs[chunk], in_slabs[slot], a_send.at[slot], a_recv.at[slot])

    def stored(slot, side):
        source, target = ((stat_left, left_next), (stat_right, right_next))[side]
        return pltpu.make_async_copy(source.at[slot], target.at[slot], store.at[slot, side])

    spare = (first_b, second, second_b, third_b, tail_b)

    def left_root(slot):
        wait_all(in_slabs[slot], a_recv.at[slot])

        def place(pair):
            upper = from_slab(in_slabs[slot][2 * pair].astype(jnp.float32))
            lower = from_slab(in_slabs[slot][2 * pair + 1].astype(jnp.float32))
            rows = pl.ds(pl.multiple_of(pair * 16, 16), 16)
            block[rows] = jnp.concatenate([upper, lower], axis=0).astype(jnp.bfloat16)

        loop(count // 2, place, unroll=2)
        excess(
            lambda columns: dot(block[...], block[columns], ((1,), (1,))), stat_left.at[slot], *spare, left_b
        )
        stored(slot, 0).start()

    def right_root(slot):
        excess(
            lambda columns: dot(block[...], block[:, columns], ((0,), (0,))), stat_right.at[slot], *spare, right_b
        )
        stored(slot, 1).start()

    def precondition(slot):
        order = block.shape[0]

        def left_side(columns):
            part = (25.0 / 16.0) * block[:, columns].astype(jnp.float32) + dot(left_b[...], block[:, columns])
            second[:, columns] = part
            half_b[:, columns] = part.astype(jnp.bfloat16)

        column_parts(order, left_side)

        def right_side(columns):
            second[:, columns] = (25.0 / 16.0) * second[:, columns] + dot(half_b[...], right_b[:, columns])

        column_parts(order, right_side)
        raw = second[...]
        widened = block[...].astype(jnp.float32)
        mean_raw = jnp.sum(raw * raw) * (1.0 / raw.size)
        mean_block = jnp.sum(widened * widened) * (1.0 / raw.size)
        scale = jnp.sqrt((mean_block + 1e-06) / (mean_raw + 1e-06))

        def cut(owner):
            rows = pl.ds(pl.multiple_of(owner * 8, 8), 8)
            ready = to_slab(second[rows] * scale).astype(jnp.bfloat16)
            width = ready.shape[1] // 2
            out_back[2 * slot][owner] = ready[:, :width]
            out_back[2 * slot + 1][owner] = ready[:, width:]

        loop(count, cut, unroll=4)

    def send_back(part):
        hand_back(here, out_back[part], in_back[part], b_send.at[part], b_recv.at[part])

    def sent_back(part):
        wait_all(out_back[part].at[pl.ds(0, count - 1)], b_send.at[part])

    def open_gather(part):
        wait_all(in_back[part], b_recv.at[part])
        base = part // 2 * back_cap
        for half, starts in zip(halves(back_cap), ((0, 3), (1, 2))):

            def one(index):
                at = half.start + index
                q[part][0, at] = in_back[part][table[2, base + at]]

            loop(half.size, one, unroll=4)
            for copy in starts:
                gather[part][copy].start()

    def forward(chunk):
        for arrived, onward in ((0, 4), (1, 5)):
            gather[chunk][arrived].wait_recv()
            gather[chunk][onward].start()

    open_chunk(0)
    attend(query, key, value, attended)
    for chunk in range(CHUNKS):
        relay(chunk)
        if chunk + 1 < CHUNKS:
            open_chunk(chunk + 1)
        else:
            loads[1].wait()
            loads[2].wait()
        finish(chunk)
    left_root(0)
    right_root(0)
    precondition(0)
    send_back(0)
    left_root(1)
    sent_back(0)
    send_back(1)
    right_root(1)
    open_gather(0)
    precondition(1)
    sent_back(1)
    send_back(2)
    forward(0)
    open_gather(1)
    sent_back(2)
    send_back(3)
    forward(1)
    for part in (2, 3):
        open_gather(part)
        forward(part)
    for part in range(PARTS):
        for copy in range(2, 6):
            gather[part][copy].wait_recv()

    def settle(number):
        place = table[3, number]
        slot, inside = place // (4 * back_cap), place % (4 * back_cap)
        relative, at = inside // back_cap, inside % back_cap
        pieces = [q[part][relative, at].astype(jnp.float32) for part in range(PARTS)]
        sides = [jnp.where(slot == 0, pieces[side], pieces[2 + side]) for side in range(2)]
        slab = jnp.concatenate(sides, axis=1)
        update_ref[number] = from_slab(slab).astype(jnp.bfloat16)

    loop(update_ref.shape[0], settle, unroll=8)
    for copies in reduce + gather:
        for copy in copies:
            copy.wait_send()
    for slot in range(2):
        wait_all(in_slabs[slot].at[pl.ds(0, count - 1)], a_send.at[slot])
        for side in range(2):
            stored(slot, side).wait()
    sent_back(3)


def step(grads, stat_left, stat_right, query, key, value, table, bounds, back_cap, count, number):
    blocks, rows, columns = grads.shape
    order = stat_left.shape[1]
    slab, thin = (2 * rows, columns // 2), (2 * rows, columns // 4)
    narrow = VMEM((order, order), jnp.bfloat16)
    wide = VMEM((order, order), jnp.float32)
    some = VMEM((count // 2,) + slab, jnp.bfloat16)
    every = VMEM((count,) + slab, jnp.bfloat16)
    slim = VMEM((count,) + thin, jnp.bfloat16)
    dma = pltpu.SemaphoreType.DMA
    near, far = pl.BlockSpec(memory_space=VMEM), pl.BlockSpec(memory_space=pl.ANY)
    return pl.pallas_call(
        functools.partial(step_kernel, bounds, back_cap, count),
        out_shape=(
            jax.ShapeDtypeStruct(stat_left.shape, jnp.float32),
            jax.ShapeDtypeStruct(stat_right.shape, jnp.float32),
            jax.ShapeDtypeStruct(grads.shape, jnp.bfloat16),
            jax.ShapeDtypeStruct(query.shape, jnp.bfloat16),
        ),
        in_specs=[pl.BlockSpec(memory_space=SMEM), near, near, near, far, far, far],
        out_specs=[far, far, near, near],
        scratch_shapes=[
            *[
                VMEM(lead + slab, jnp.bfloat16)
                for cap in [end - begin for begin, end in zip((0,) + bounds, bounds)]
                for lead in ((4, cap), (cap,), (cap,), (cap,), (cap,))
            ],
            *[some] * 4, *[every] * 2, *[slim] * (2 * PARTS),
            *[VMEM((4, back_cap) + thin, jnp.bfloat16)] * PARTS,
            VMEM((bounds[-1],) + slab, jnp.bfloat16),
            VMEM(grads.shape, jnp.bfloat16), VMEM(stat_left.shape, jnp.float32), VMEM(stat_left.shape, jnp.float32),
            narrow, narrow, wide, narrow, narrow, narrow, narrow, narrow, narrow,
            dma((CHUNKS, 6)), dma((CHUNKS, 6)), dma((PARTS, 6)), dma((PARTS, 6)),
            dma((2,)), dma((2,)), dma((PARTS,)), dma((PARTS,)), dma((3,)), dma((2, 2)),
        ],
        compiler_params=pltpu.CompilerParams(
            collective_id=number, has_side_effects=True, vmem_limit_bytes=56 * 2**20
        ),
    )(table, query, key, value, grads, stat_left, stat_right)


def table_kernel(bounds, back_cap, count, assign_ref, table, over):
    blocks = assign_ref.shape[1]
    pairs = count // 2
    slots = 8 * count
    width = table.shape[1]
    here = lax.axis_index("dp")
    wide = lax.broadcast_in_dim(assign_ref[...], (width, blocks), (0, 1))
    slot = wide.T
    number = lax.broadcasted_iota(jnp.int32, (blocks, width), 0)
    lane = lax.broadcasted_iota(jnp.int32, (blocks, width), 1)
    inside = lane % pairs
    chunk = (lane // pairs) % CHUNKS
    replica = lane // (CHUNKS * pairs)
    listed = replica * (CHUNKS * pairs) + 4 * inside + 2 * (chunk % 2) + chunk // 2
    hit = jnp.where(slot == listed, 1.0, 0.0)
    taken = jnp.sum(hit, axis=0, keepdims=True)
    before = lax.broadcasted_iota(jnp.int32, (width, width), 0)
    after = lax.broadcasted_iota(jnp.int32, (width, width), 1)
    taken_b = lax.broadcast_in_dim(taken, (8, width), (0, 1)).astype(jnp.bfloat16)

    def ranks(group):
        counts = jnp.where((before < after) & (before // group == after // group), 1.0, 0.0).astype(jnp.bfloat16)
        rank = dot(taken_b, counts)[0:1]
        return rank, jnp.sum(hit * rank, axis=1, keepdims=True).astype(jnp.int32)

    rank, own_rank = ranks(CHUNKS * pairs)
    _, back_rank = ranks(2 * pairs)
    own_chunk = 2 * (slot % 2) + (slot // 2) % 2
    own_replica = slot // (CHUNKS * pairs)
    place = own_replica * bounds[-1] + own_rank
    bound = jnp.full(own_chunk.shape, bounds[0], jnp.int32)
    for chunk_number in range(1, CHUNKS):
        bound = jnp.where(own_chunk == chunk_number, bounds[chunk_number], bound)
    table[...] = jnp.zeros(table.shape, jnp.int32)
    table[0:1] = jnp.sum(jnp.where(place == lane, number, 0), axis=0, keepdims=True)
    table[1:2] = jnp.where(taken > 0.0, rank.astype(jnp.int32), -1)
    owner = (slot // 2) % count
    back = (slot % 2) * back_cap + back_rank
    mine = jnp.where(own_replica == here, back, -1)
    table[2:3] = jnp.sum(jnp.where(mine == lane, owner, 0), axis=0, keepdims=True)
    relative = (own_replica - here + 4) % 4
    found = (slot % 2) * (4 * back_cap) + relative * back_cap + back_rank
    table[3:4, 0:blocks] = found.T[0:1]
    over[0, 0] = jnp.maximum(jnp.max(own_rank - bound), jnp.max(back_rank) - back_cap) + 1


def make_table(assign, bounds, back_cap, count):
    width = 8 * count
    return pl.pallas_call(
        functools.partial(table_kernel, bounds, back_cap, count),
        out_shape=(jax.ShapeDtypeStruct((8, width), jnp.int32), jax.ShapeDtypeStruct((1, 1), jnp.int32)),
        in_specs=[pl.BlockSpec(memory_space=VMEM)],
        out_specs=(pl.BlockSpec(memory_space=VMEM), pl.BlockSpec(memory_space=SMEM)),
        compiler_params=pltpu.CompilerParams(vmem_limit_bytes=32 * 2**20),
    )(assign.reshape(1, -1))


def body(partial_grads, stat_left, stat_right, assign, query_vectors, key_vectors, value_vectors):
    count = lax.axis_size("mp")
    arrays = (
        partial_grads[0], stat_left[0], stat_right[0], query_vectors, key_vectors, value_vectors,
    )
    pairs = count // 2
    tight = tuple(pairs * part // 4 for part in (3, 5, 7, 9)), 5 * count // 8
    full = tuple(pairs * part for part in (1, 2, 3, 4)), count
    table, over = make_table(assign, *tight, count)
    left_next, right_next, update, attended = lax.cond(
        over[0, 0] <= 0,
        lambda: step(*arrays, table, *tight, count, 0),
        lambda: step(*arrays, make_table(assign, *full, count)[0], *full, count, 1),
    )
    return (left_next[None], right_next[None], update, attended)


def solution(mesh):
    placed = (
        P("dp", None, "mp", None),
        P("dp", "mp", None, None),
        P("dp", "mp", None, None),
        P(),
        P("dp", "mp"),
        P("dp", "mp"),
        P("dp", "mp"),
    )
    return jax.shard_map(
        body,
        mesh=mesh,
        in_specs=placed,
        out_specs=(
            P("dp", "mp", None, None),
            P("dp", "mp", None, None),
            P(None, "mp", None),
            P("dp", "mp"),
        ),
        check_vma=False,
    )
```
